512 devices in a mesh: dp: 16 (over z), expert: 32 (over x, y, core).
Axes of the slice: x: 4, y: 4, z: 16, core: 2. Of those that a mesh axis runs over, the one named last changes fastest.
Arguments:
- tokens: bfloat16 [65536, 1024], P(('dp', 'expert')), may hold values from -6 to 6
- routes: int32 [65536, 8], P(('dp', 'expert')), may hold values from 0 to 63, all different within a row; in each aligned block of 128 rows (0 to 127, 128 to 255, ...) at most 24 rows name the same one
- route_gates: float32 [65536, 8], P(('dp', 'expert')), may hold values from 0.1 to 9
- route_cotangent: bfloat16 [65536, 8, 384], P(('dp', 'expert')), may hold values from -4 to 4
- gate_up: bfloat16 [1024, 64, 768], P('dp', 'expert'), may hold values from -0.1875 to 0.1875
Outputs:
- grad_tokens: bfloat16 [65536, 1024], P(('dp', 'expert'))
- grad_gate_up: bfloat16 [1024, 64, 768], P('dp', 'expert')
- load: float32 [64], P('expert')
The draws below stay inside these ranges and needn't reach their ends.
Inputs may be any that keep to these rules, and one draw needn't show every extreme that they name: `routes`: each token names 8 different experts. Among the 128 rows of one device, no expert is named by more than 24 rows, a bound that some block reaches.
All inputs are finite; a program needn't handle non-finite values.
Results may differ from the reference program's by a relative error of at most 0.023.
Values may be sent and summed in bfloat16 or wider, within the bound.
No kernel may reach another device: no remote copies, remote signals or barrier semaphores. Data moves between devices by JAX's collectives and lax.ppermute only.
A program may use at most 64 MiB of HBM per device.

```python
import math
import jax
import jax.numpy as jnp
import numpy as np
from jax import lax

D = 1024
FF = 384
TOPK = 8
TOK_DEV = 128
EXPERTS = 64
TOKENS = 65536
CAP = 24
N_DP = 16
N_EXPERT = 32


def draw_route_gates(key, part):
    key = jax.random.fold_in(key, 7)
    base = jax.random.uniform(key, (TOKENS, TOPK), jnp.float32, 0.1, 1.0)
    position = jnp.arange(TOKENS, dtype=jnp.float32) / TOKENS
    rising = 1.0 + 2.0 * position
    return base * rising[:, None]


def level_of(rng, extent, cuts, low, high):
    gain = 1.0
    for axis_at, parts in cuts:
        heights = jax.random.uniform(jax.random.fold_in(jax.random.fold_in(rng, 6), axis_at), (parts,), jnp.float32, low / len(cuts), high / len(cuts))
        gain = gain * jnp.repeat(jnp.exp(heights), extent[axis_at] // parts).reshape((-1,) + (1,) * (len(extent) - 1 - axis_at))
    return gain


def deal_out(key, own, number, rows, number_of, top, reach, skew):
    order = jax.random.permutation(key, number_of)
    crowded, usual = load_shares(number_of, rows * top, reach, skew, True), load_shares(number_of, rows * top, reach, skew, False)
    places = jnp.arange(number_of)

    def named(tallies, offset_by):
        used = int((tallies > 0).sum())
        fixed = max(1, used // 4)
        shifted = fixed + (places - fixed + offset_by * (used - fixed)) % max(1, number_of - fixed)
        return jnp.zeros((number_of,), jnp.int32).at[order[jnp.where(places < fixed, places, shifted)]].set(jnp.asarray(tallies, jnp.int32))

    tallies = jnp.where(number % 4 == 0, named(crowded, number // 4), named(usual, number - number // 4 - 1))
    mixed = jax.random.permutation(jax.random.fold_in(own, 3), number_of)
    source_of, taker = mixed[0:number_of // 2 * 2:2], mixed[1:number_of // 2 * 2:2]
    room = jnp.minimum(tallies[source_of] - 1, reach - tallies[taker]) // 2
    room = jnp.where((source_of == order[0]) | (taker == order[0]) | (tallies[taker] == 0), 0, jnp.maximum(room, 0))
    shifted = jax.random.randint(jax.random.fold_in(own, 4), (number_of // 2,), 0, 1 << 20) % (room + 1)
    tallies = tallies.at[source_of].add(-shifted).at[taker].add(shifted)
    items = jnp.searchsorted(jnp.cumsum(tallies), jnp.arange(rows * top), side="right").astype(jnp.int32)
    listing = items.reshape(top, rows).T
    listing = listing[jax.random.permutation(jax.random.fold_in(own, 1), rows)]
    offset_by = jax.random.randint(jax.random.fold_in(own, 2), (rows, 1), 0, top)
    return jnp.take_along_axis(listing, (jnp.arange(top)[None, :] + offset_by) % top, axis=1)


def load_shares(amount, total, limit, slope, full):
    weights = [(1 << 20) // math.isqrt(standing ** slope) + 1 for standing in range(1, amount + 1)]
    largest = limit if full else min(limit, max(-(-total // amount), total * weights[0] // sum(weights)))
    least = 1 if total - largest >= amount - 1 else 0
    holding, spare = [largest] + [least] * (amount - 1), total - largest - least * (amount - 1)
    while spare > 0:
        candidates = [i for i in range(1, amount) if holding[i] < largest] or [i for i in range(1, amount) if holding[i] < limit]
        whole, remaining = sum([weights[i] for i in candidates]), spare
        for i in candidates:
            addition = min(limit - holding[i], max(1, remaining * weights[i] // whole), spare)
            holding[i] = holding[i] + addition
            spare = spare - addition
    return np.array(holding)


def centred(stream_key, extent, spread, most, shards=(), held_as=jnp.bfloat16):
    factor_of = level_of(stream_key, extent, shards, -0.22, 0.18) if shards else 1.0
    values = jax.random.normal(stream_key, extent, jnp.float32) * spread * factor_of
    return jnp.minimum(jnp.maximum(values, -most), most).astype(held_as)


def setup_inputs(seed: int = 0) -> dict:
    arg_keys = jax.random.split(jax.random.key(seed), 6)
    tokens = centred(arg_keys[0], (TOKENS, D), 1.0, 6.0, ((0, 512),))
    routes_keys = jax.random.split(jax.random.fold_in(arg_keys[1], 1), TOKENS // TOK_DEV)
    routes_turns = jax.random.permutation(jax.random.fold_in(arg_keys[1], 3), TOKENS // TOK_DEV)
    routes = jax.vmap(lambda own, number: deal_out(jax.random.fold_in(arg_keys[1], 2), own, number, TOK_DEV, EXPERTS, TOPK, CAP, 2))(routes_keys, routes_turns).reshape((TOKENS, TOPK))
    route_gates = draw_route_gates(jax.random.fold_in(arg_keys[5], 71), 0)
    route_cotangent = centred(arg_keys[3], (TOKENS, TOPK, FF), 0.25, 4.0, ((0, 512),))
    gate_up = centred(arg_keys[4], (D, EXPERTS, 2 * FF), D ** -0.5, 0.1875, ((0, 16), (1, 32)))
    return dict(tokens=tokens, routes=routes, route_gates=route_gates, route_cotangent=route_cotangent, gate_up=gate_up)


def swiglu_grads(pre, cotangent, width):
    gate = pre[..., :width]
    upper = pre[..., width:]
    sigma = jax.nn.sigmoid(gate)
    scaled = cotangent.astype(jnp.float32)
    d_gate = scaled * upper * sigma * (1.0 + gate * (1.0 - sigma))
    d_upper = scaled * gate * sigma
    return jnp.concatenate([d_gate, d_upper], axis=-1).astype(jnp.bfloat16)


def reference(tokens, routes, route_gates, route_cotangent, gate_up):
    block = N_EXPERT * TOK_DEV
    slots = N_EXPERT * CAP
    count_routes = block * TOPK
    scaled = (route_gates[:, :, None] * route_cotangent.astype(jnp.float32)).astype(jnp.bfloat16)
    gate_mark = lax.optimization_barrier(route_gates.astype(jnp.bfloat16)).astype(jnp.float32)
    weights = jnp.transpose(gate_up, (1, 0, 2))
    labels = jnp.arange(EXPERTS, dtype=jnp.int32)

    def expert_pass(operands):
        weight, rows, cotangent = operands
        pre = jnp.dot(rows, weight, preferred_element_type=jnp.float32)
        grad_pre = swiglu_grads(pre, cotangent, FF)
        grad_rows = jnp.dot(grad_pre, weight.T, preferred_element_type=jnp.float32).astype(jnp.bfloat16)
        grad_weight = jnp.dot(rows.T, grad_pre, preferred_element_type=jnp.float32)
        return grad_rows, grad_weight.astype(jnp.bfloat16)

    def one_group(carry, index):
        total_grad, total_count = carry
        start = (index * block).astype(jnp.int32)
        tok_block = lax.dynamic_slice_in_dim(tokens, start, block, 0)
        route_block = lax.dynamic_slice_in_dim(routes, start, block, 0).reshape(-1)
        mark_block = lax.dynamic_slice_in_dim(gate_mark, start, block, 0).reshape(-1)
        cot_block = lax.dynamic_slice_in_dim(scaled, start, block, 0).reshape(count_routes, FF)
        table = (route_block[:, None] == labels[None, :]).astype(jnp.int32)
        earlier = jnp.sum((jnp.cumsum(table, axis=0) - table) * table, axis=1)
        slot_index = (route_block * slots + earlier).astype(jnp.int32)
        owner = jnp.full((EXPERTS * slots,), count_routes, jnp.int32).at[slot_index].set(jnp.arange(count_routes, dtype=jnp.int32))
        valid = owner < count_routes
        safe_owner = jnp.where(valid, owner, 0).astype(jnp.int32)
        rows = jnp.where(valid[:, None], tok_block[safe_owner // TOPK], jnp.zeros((), tokens.dtype))
        cots = jnp.where(valid[:, None], cot_block[safe_owner], jnp.zeros((), scaled.dtype))
        grad_rows, grad_weight = lax.map(expert_pass, (weights, rows.reshape(EXPERTS, slots, D), cots.reshape(EXPERTS, slots, FF)))
        picked = grad_rows.reshape(EXPERTS * slots, D)[slot_index].astype(jnp.float32)
        grad_block = jnp.sum(picked.reshape(block, TOPK, D), axis=1).astype(jnp.bfloat16)
        sums = jnp.sum(table.astype(jnp.float32) * mark_block[:, None], axis=0)
        new_carry = (total_grad + grad_weight.astype(jnp.float32), total_count + sums)
        return new_carry, grad_block

    init = (jnp.zeros((EXPERTS, D, 2 * FF), jnp.float32), jnp.zeros((EXPERTS,), jnp.float32))
    (total_grad, total_count), blocks = lax.scan(one_group, init, jnp.arange(N_DP, dtype=jnp.int32))
    grad_tokens = blocks.reshape(TOKENS, D)
    grad_gate_up = jnp.transpose(total_grad, (1, 0, 2)).astype(jnp.bfloat16)
    load = total_count * (EXPERTS / (TOKENS * TOPK))
    return grad_tokens, grad_gate_up, load
```

```python
import functools

import jax
import jax.numpy as jnp
from jax import lax
from jax.experimental import pallas as pl
from jax.experimental.pallas import tpu as pltpu
from jax.sharding import PartitionSpec as P

F32 = jnp.float32
BF16 = jnp.bfloat16
VMEM_LIMIT = 48 * 1024 * 1024


def iota(shape, dim):
    return lax.broadcasted_iota(jnp.int32, shape, dim)


def dot(a, b, contract=((1,), (0,))):
    return lax.dot_general(a, b, (contract, ((), ())), preferred_element_type=F32)


def plan(routes_row, tok_count, topk, per_device, devices, cap):
    experts, count = per_device * devices, tok_count * topk
    row = iota((experts, 1), 0)
    expert = (row % devices) * per_device + row // devices
    table = routes_row == expert
    spread = (iota((tok_count, count), 1) // topk == iota((tok_count, count), 0)).astype(BF16)
    tok_table = dot(table.astype(BF16), spread, ((1,), (1,)))
    before = (iota((tok_count, tok_count), 0) < iota((tok_count, tok_count), 1)).astype(BF16)
    earlier = dot(tok_table.astype(BF16), before)
    tok_slot = jnp.where(tok_table > 0.5, earlier, -1.0).astype(jnp.int32)
    route_earlier = dot(earlier.astype(BF16), spread)
    slots = jnp.where(table, (row * cap).astype(F32) + route_earlier, 0.0)
    slot = jnp.sum(slots, axis=0, keepdims=True).astype(jnp.int32)
    return table, slot, tok_slot


def token_kernel(per_device, devices, cap, routes_ref, gates_ref, tokens_ref, rows_ref, picks_ref, slot_ref, sums_ref):
    tok_count, model = tokens_ref.shape
    topk = routes_ref.shape[1] // tok_count
    experts = per_device * devices
    table, slot, tok_slot = plan(routes_ref[...], tok_count, topk, per_device, devices, cap)
    slot_ref[...] = slot
    mark = gates_ref[...].astype(BF16).astype(F32)
    sums_ref[...] = jnp.sum(jnp.where(table, mark, 0.0), axis=1, keepdims=True)
    hits = tok_slot[:, None, :] == iota((experts, cap, tok_count), 1)
    picks = hits.astype(F32).reshape(experts * cap, tok_count).astype(BF16)
    size = devices * cap
    tokens = tokens_ref[...]
    for j in range(per_device):
        mine = picks[j * size : (j + 1) * size]
        picks_ref[:, j * tok_count : (j + 1) * tok_count] = mine
        rows_ref[:, j * model : (j + 1) * model] = dot(mine, tokens).astype(BF16)


def cot_kernel(per_device, slot_ref, gates_ref, cot_ref, out_ref):
    size = out_ref.shape[0]
    count, width = cot_ref.shape
    step = 128
    slot, gates = slot_ref[...], gates_ref[...]
    for j in range(per_device):
        for i in range(size // step):
            hit = slot == iota((step, 1), 0) + (j * size + i * step)
            gate = jnp.sum(jnp.where(hit, gates, 0.0), axis=1, keepdims=True)
            rows = dot(hit.astype(F32).astype(BF16), cot_ref[...])
            out_ref[i * step : (i + 1) * step, j * width : (j + 1) * width] = (rows * gate).astype(BF16)


def grad_kernel(rows_ref, cot_ref, w_ref, gp_ref, gw_ref):
    size, model = rows_ref.shape
    width = cot_ref.shape[1]
    step = 256
    for i in range(size // step):
        part = pl.ds(i * step, step)
        pre = dot(rows_ref[part, :], w_ref[...])
        gate, upper = pre[:, :width], pre[:, width:]
        sigma = jax.nn.sigmoid(gate)
        scaled = cot_ref[part, :].astype(F32)
        common = scaled * sigma
        gp_ref[part, :width] = (common * upper * (1.0 + gate * (1.0 - sigma))).astype(BF16)
        gp_ref[part, width:] = (common * gate).astype(BF16)
    for i in range(model // step):
        part = pl.ds(i * step, step)
        gw_ref[part, :] = dot(rows_ref[:, part], gp_ref[...], ((0,), (0,))).astype(BF16)


def route_kernel(gp_ref, w_ref, out_ref):
    size = gp_ref.shape[0]
    step = 256
    for i in range(size // step):
        part = pl.ds(i * step, step)
        out_ref[part, :] = dot(gp_ref[part, :], w_ref[...], ((1,), (1,))).astype(BF16)


def sum_kernel(per_device, picks_ref, back_ref, out_ref):
    tok_count, model = out_ref.shape
    total = jnp.zeros((tok_count, model), F32)
    for j in range(per_device):
        picks = picks_ref[:, j * tok_count : (j + 1) * tok_count]
        total += dot(picks, back_ref[:, j * model : (j + 1) * model], ((0,), (0,)))
    out_ref[...] = total.astype(BF16)


def call(kernel, outs, *args, cost):
    whole = pl.BlockSpec(memory_space=pltpu.VMEM)
    return pl.pallas_call(
        kernel,
        out_shape=[jax.ShapeDtypeStruct(s, t) for s, t in outs],
        in_specs=[whole] * len(args),
        out_specs=[whole] * len(outs),
        compiler_params=pltpu.CompilerParams(vmem_limit_bytes=VMEM_LIMIT),
        cost_estimate=cost,
    )(*args)


def estimate(flops, moved):
    return pl.CostEstimate(flops=flops, bytes_accessed=moved, transcendentals=0)


def body(tokens, routes, route_gates, route_cotangent, gate_up):
    tok_count, topk = routes.shape
    width = route_cotangent.shape[2]
    model = tokens.shape[1]
    channels, per_device, hidden = gate_up.shape
    devices = lax.axis_size("expert")
    data_ways = lax.axis_size("dp")
    cap = 3 * tok_count * topk // (2 * per_device * devices)
    size, count = devices * cap, tok_count * topk

    lift = 2.0**18
    weights = gate_up.reshape(channels, per_device * hidden)
    sent = (weights.astype(F32) * lift).astype(jnp.float16)

    routes_row = routes.reshape(1, count)
    gates_row = route_gates.reshape(1, count)
    rows, picks, slot, sums = call(
        functools.partial(token_kernel, per_device, devices, cap),
        [((size, per_device * model), BF16), ((size, per_device * tok_count), BF16), ((1, count), jnp.int32), ((per_device * devices, 1), F32)],
        routes_row,
        gates_row,
        tokens,
        cost=estimate(2 * size * per_device * tok_count * model, 2 * size * per_device * model),
    )
    got_rows = lax.all_to_all(rows, "expert", split_axis=0, concat_axis=0, tiled=True)
    (cots,) = call(
        functools.partial(cot_kernel, per_device),
        [((size, per_device * width), BF16)],
        slot,
        gates_row,
        route_cotangent.reshape(count, width),
        cost=estimate(2 * size * per_device * count * width, 2 * size * per_device * width),
    )
    got_cots = lax.all_to_all(cots, "expert", split_axis=0, concat_axis=0, tiled=True)
    everyone = lax.psum(sums.reshape(-1), ("dp", "expert"))
    gathered = lax.all_gather(sent, "dp", axis=0, tiled=True)
    full = (gathered.astype(F32) * (1.0 / lift)).astype(BF16)

    cut = [
        pl.BlockSpec((size, model), lambda j: (0, j)),
        pl.BlockSpec((size, width), lambda j: (0, j)),
        pl.BlockSpec((model, hidden), lambda j: (0, j)),
        pl.BlockSpec((size, hidden), lambda j: (0, j)),
    ]
    params = pltpu.CompilerParams(vmem_limit_bytes=VMEM_LIMIT, dimension_semantics=("arbitrary",))
    work = 2 * per_device * size * model * hidden
    grad_pre, part = pl.pallas_call(
        grad_kernel,
        grid=(per_device,),
        in_specs=[cut[0], cut[1], cut[2]],
        out_specs=[cut[3], cut[2]],
        out_shape=[
            jax.ShapeDtypeStruct((size, per_device * hidden), BF16),
            jax.ShapeDtypeStruct((model, per_device * hidden), BF16),
        ],
        compiler_params=params,
        cost_estimate=estimate(2 * work, 12 * size * model),
    )(got_rows, got_cots, full)
    mine = lax.psum_scatter(part, "dp", scatter_dimension=0, tiled=True)
    back = pl.pallas_call(
        route_kernel,
        grid=(per_device,),
        in_specs=[cut[3], cut[2]],
        out_specs=cut[0],
        out_shape=jax.ShapeDtypeStruct((size, per_device * model), BF16),
        compiler_params=params,
        cost_estimate=estimate(work, 12 * size * model),
    )(grad_pre, full)
    returned = lax.all_to_all(back, "expert", split_axis=0, concat_axis=0, tiled=True)
    (grad_tokens,) = call(
        functools.partial(sum_kernel, per_device),
        [((tok_count, model), BF16)],
        picks,
        returned,
        cost=estimate(2 * size * per_device * tok_count * model, 2 * size * per_device * model),
    )
    sums_here = lax.dynamic_index_in_dim(everyone.reshape(per_device, devices), lax.axis_index("expert"), 1, keepdims=False)
    load = sums_here * (per_device / (tok_count * topk * data_ways))
    return (grad_tokens, mine.reshape(channels, per_device, hidden), load)


def solution(mesh):
    in_specs = (
        P(("dp", "expert"), None),
        P(("dp", "expert"), None),
        P(("dp", "expert"), None),
        P(("dp", "expert"), None, None),
        P("dp", "expert", None),
    )
    out_specs = (P(("dp", "expert"), None), P("dp", "expert", None), P("expert"))
    return jax.shard_map(body, mesh=mesh, in_specs=in_specs, out_specs=out_specs, check_vma=False)
```

```python
import functools

import jax
import jax.numpy as jnp
from jax import lax
from jax.experimental import pallas as pl
from jax.experimental.pallas import tpu as pltpu
from jax.sharding import PartitionSpec as P

F32 = jnp.float32
BF16 = jnp.bfloat16
VMEM_LIMIT = 48 * 1024 * 1024


def iota(shape, dim):
    return lax.broadcasted_iota(jnp.int32, shape, dim)


def dot(a, b, contract=((1,), (0,))):
    return lax.dot_general(a, b, (contract, ((), ())), preferred_element_type=F32)


def split3(x):
    high = x.astype(BF16)
    rest = x - high.astype(F32)
    middle = rest.astype(BF16)
    return high, middle, (rest - middle.astype(F32)).astype(BF16)


def pack_kernel(per_device, devices, cap, routes_ref, gates_ref, tokens_hbm, cot_hbm, out_ref, picks_ref, sums_ref, tokens_ref, cot_ref, sems):
    topk, tok_count = routes_ref.shape
    model, width = tokens_ref.shape[1], cot_ref.shape[1]
    count, experts = tok_count * topk, per_device * devices
    size = devices * cap
    copies = [
        pltpu.make_async_copy(tokens_hbm, tokens_ref, sems.at[0]),
        pltpu.make_async_copy(cot_hbm, cot_ref, sems.at[1]),
    ]
    for copy in copies:
        copy.start()

    spread = (iota((tok_count, count), 1) // topk == iota((tok_count, count), 0)).astype(F32).astype(BF16)
    own = iota((topk, count), 1) % topk == iota((topk, count), 0)
    parts = [routes_ref[...].astype(F32).astype(BF16), *split3(gates_ref[...])]
    wide = [jnp.sum(jnp.where(own, dot(part, spread), 0.0), axis=0, keepdims=True) for part in parts]
    routes, gates = wide[0].astype(jnp.int32), (wide[1] + wide[2]) + wide[3]

    row = iota((experts, 1), 0)
    table = routes == (row % devices) * per_device + row // devices
    tok_table = dot(table.astype(F32).astype(BF16), spread, ((1,), (1,)))
    before = (iota((tok_count, tok_count), 0) < iota((tok_count, tok_count), 1)).astype(F32).astype(BF16)
    earlier = dot(tok_table.astype(BF16), before)
    tok_slot = jnp.where(tok_table > 0.5, earlier, -1.0).astype(jnp.int32)
    slots = jnp.where(table, (row * cap).astype(F32) + dot(earlier.astype(BF16), spread), 0.0)
    slot = jnp.sum(slots, axis=0, keepdims=True).astype(jnp.int32)

    mark = gates.astype(BF16).astype(F32)
    sums = jnp.sum(jnp.where(table, mark, 0.0), axis=1, keepdims=True)
    for j in range(per_device):
        sums_ref[:, j * 128 : (j + 1) * 128] = jnp.broadcast_to(sums[j * devices : (j + 1) * devices], (devices, 128))

    hits = tok_slot[:, None, :] == iota((experts, cap, tok_count), 1)
    picks_ref[...] = hits.astype(F32).reshape(experts * cap, tok_count).astype(BF16)
    step = 256
    copies[0].wait()
    for j in range(per_device):
        for i in range(0, size, step):
            rows = dot(picks_ref[j * size + i : j * size + i + step, :], tokens_ref[...])
            out_ref[i : i + step, j * model : (j + 1) * model] = rows.astype(BF16)
    copies[1].wait()
    for j in range(per_device):
        for i in range(0, size, step):
            hit = slot == iota((step, 1), 0) + (j * size + i)
            gate = jnp.sum(jnp.where(hit, gates, 0.0), axis=1, keepdims=True)
            rows = dot(hit.astype(F32).astype(BF16), cot_ref[...])
            at = per_device * model + j * width
            out_ref[i : i + step, at : at + width] = (rows * gate).astype(BF16)


def grad_kernel(per_device, got_hbm, w_hbm, gp_ref, gw_hbm, got_ref, w_ref, gw_ref, sems):
    size, hidden, model = gp_ref.shape[0], gp_ref.shape[1] // per_device, w_ref.shape[0]
    width = hidden // 2
    step = 256
    tiles = size // step
    rows = [pl.ds(i * step, step) for i in range(tiles)]
    columns = [pl.ds(j * hidden, hidden) for j in range(per_device)]
    w_in = [
        pltpu.make_async_copy(w_hbm.at[:, columns[j]], w_ref.at[:, columns[j]], sems.at[j]) for j in range(per_device)
    ]
    got_in = [
        pltpu.make_async_copy(got_hbm.at[rows[i], :], got_ref.at[rows[i], :], sems.at[per_device + i])
        for i in range(tiles)
    ]
    for copy in (w_in[0], *got_in, *w_in[1:]):
        copy.start()
    outs = []
    for j in range(per_device):
        w_in[j].wait()
        at = j * hidden
        for i in range(tiles):
            if j == 0:
                got_in[i].wait()
            pre = dot(got_ref[rows[i], j * model : (j + 1) * model], w_ref[:, columns[j]])
            gate, upper = pre[:, :width], pre[:, width:]
            sigma = jax.nn.sigmoid(gate)
            first = per_device * model + j * width
            common = got_ref[rows[i], first : first + width].astype(F32) * sigma
            gp_ref[rows[i], at : at + width] = (common * upper * (1.0 + gate * (1.0 - sigma))).astype(BF16)
            gp_ref[rows[i], at + width : at + hidden] = (common * gate).astype(BF16)
        for i in range(0, model, step):
            part = got_ref[:, j * model + i : j * model + i + step]
            gw_ref[i : i + step, columns[j]] = dot(part, gp_ref[:, columns[j]], ((0,), (0,))).astype(BF16)
        copy = pltpu.make_async_copy(gw_ref.at[:, columns[j]], gw_hbm.at[:, columns[j]], sems.at[per_device + tiles + j])
        copy.start()
        outs.append(copy)
    for copy in outs:
        copy.wait()


def route_kernel(gp_ref, w_ref, out_ref):
    step = 256
    for i in range(0, gp_ref.shape[0], step):
        out_ref[i : i + step, :] = dot(gp_ref[i : i + step, :], w_ref[...], ((1,), (1,))).astype(BF16)


def sum_kernel(per_device, picks_ref, back_ref, out_ref):
    tok_count, model = out_ref.shape
    size = back_ref.shape[0]
    total = jnp.zeros((tok_count, model), F32)
    for j in range(per_device):
        total += dot(picks_ref[j * size : (j + 1) * size, :], back_ref[:, j * model : (j + 1) * model], ((0,), (0,)))
    out_ref[...] = total.astype(BF16)


def call(kernel, outs, args, in_specs=None, out_specs=None, grid=(), scratch=(), flops=0, moved=0):
    whole = pl.BlockSpec(memory_space=pltpu.VMEM)
    return pl.pallas_call(
        kernel,
        grid=grid,
        out_shape=[jax.ShapeDtypeStruct(s, t) for s, t in outs],
        in_specs=in_specs or [whole] * len(args),
        out_specs=out_specs or [whole] * len(outs),
        scratch_shapes=scratch,
        compiler_params=pltpu.CompilerParams(vmem_limit_bytes=VMEM_LIMIT),
        cost_estimate=pl.CostEstimate(flops=flops, bytes_accessed=moved, transcendentals=0),
    )(*args)


def body(tokens, routes, route_gates, route_cotangent, gate_up):
    tok_count, topk = routes.shape
    width = route_cotangent.shape[2]
    model = tokens.shape[1]
    channels, per_device, hidden = gate_up.shape
    devices = lax.axis_size("expert")
    data_ways = lax.axis_size("dp")
    experts = per_device * devices
    cap = 3 * tok_count * topk // (2 * experts)
    size, count = devices * cap, tok_count * topk
    lanes = per_device * (model + width)
    vmem, anywhere = pl.BlockSpec(memory_space=pltpu.VMEM), pl.BlockSpec(memory_space=pl.ANY)

    lift = 2.0**18
    sent = (gate_up.astype(F32) * lift).astype(jnp.float16).reshape(channels, per_device * hidden)

    packed, picks, sums = call(
        functools.partial(pack_kernel, per_device, devices, cap),
        [((size, lanes), BF16), ((per_device * size, tok_count), BF16), ((devices, per_device * 128), F32)],
        [routes.T, route_gates.T, tokens, route_cotangent.reshape(count, width)],
        in_specs=[vmem, vmem, anywhere, anywhere],
        scratch=[pltpu.VMEM((tok_count, model), BF16), pltpu.VMEM((count, width), BF16), pltpu.SemaphoreType.DMA((2,))],
        flops=2 * per_device * size * (tok_count * model + count * width),
        moved=2 * size * lanes,
    )
    got = lax.all_to_all(packed, "expert", split_axis=0, concat_axis=0, tiled=True)
    gathered = lax.all_gather(sent, "dp", axis=0, tiled=True)
    full = (gathered.astype(F32) * (1.0 / lift)).astype(BF16)

    work = 2 * per_device * size * model * hidden
    grad_pre, part = call(
        functools.partial(grad_kernel, per_device),
        [((size, per_device * hidden), BF16), ((model, per_device * hidden), BF16)],
        [got, full],
        in_specs=[anywhere, anywhere],
        out_specs=[vmem, anywhere],
        scratch=[
            pltpu.VMEM((size, lanes), BF16),
            pltpu.VMEM((model, per_device * hidden), BF16),
            pltpu.VMEM((model, per_device * hidden), BF16),
            pltpu.SemaphoreType.DMA((2 * per_device + size // 256,)),
        ],
        flops=2 * work,
        moved=12 * size * model,
    )
    mine = lax.psum_scatter(part, "dp", scatter_dimension=0, tiled=True)
    (back,) = call(
        route_kernel,
        [((size, per_device * model), BF16)],
        [grad_pre, full],
        in_specs=[pl.BlockSpec((size, hidden), lambda j: (0, j)), pl.BlockSpec((model, hidden), lambda j: (0, j))],
        out_specs=[pl.BlockSpec((size, model), lambda j: (0, j))],
        grid=(per_device,),
        flops=work,
        moved=12 * size * model,
    )
    returned = lax.all_to_all(back, "expert", split_axis=0, concat_axis=0, tiled=True)
    (grad_tokens,) = call(
        functools.partial(sum_kernel, per_device),
        [((tok_count, model), BF16)],
        [picks, returned],
        flops=2 * per_device * size * tok_count * model,
        moved=4 * size * model,
    )

    here = jnp.sum(lax.all_to_all(sums, "expert", split_axis=0, concat_axis=0, tiled=True), axis=0, keepdims=True)
    heard = lax.all_to_all(jnp.tile(here, (data_ways, 1)), "dp", split_axis=0, concat_axis=0, tiled=True)
    totals = jnp.sum(heard, axis=0).reshape(per_device, 128)[:, 0]
    load = totals * (per_device / (tok_count * topk * data_ways))
    return (grad_tokens, mine.reshape(channels, per_device, hidden), load)


def solution(mesh):
    in_specs = (
        P(("dp", "expert"), None),
        P(("dp", "expert"), None),
        P(("dp", "expert"), None),
        P(("dp", "expert"), None, None),
        P("dp", "expert", None),
    )
    out_specs = (P(("dp", "expert"), None), P("dp", "expert", None), P("expert"))
    return jax.shard_map(body, mesh=mesh, in_specs=in_specs, out_specs=out_specs, check_vma=False)
```

```python
import functools

import jax
import jax.numpy as jnp
from jax import lax
from jax.experimental import pallas as pl
from jax.experimental.pallas import tpu as pltpu
from jax.sharding import PartitionSpec as P

F32 = jnp.float32
BF16 = jnp.bfloat16
VMEM_LIMIT = 60 * 1024 * 1024


def iota(shape, dim):
    return lax.broadcasted_iota(jnp.int32, shape, dim)


def dot(a, b, contract=((1,), (0,))):
    return lax.dot_general(a, b, (contract, ((), ())), preferred_element_type=F32)


def split3(x):
    high = x.astype(BF16)
    rest = x - high.astype(F32)
    middle = rest.astype(BF16)
    return high, middle, (rest - middle.astype(F32)).astype(BF16)


def pack_kernel(
    per_device, devices, cap, routes_hbm, gates_hbm, tokens_hbm, cot_hbm, out_hbm, picks_ref, sums_ref, routes_ref, gates_ref, tokens_ref, cot_ref, out_ref, sems
):
    topk, tok_count = routes_ref.shape
    model, width = tokens_ref.shape[1], cot_ref.shape[1]
    count, experts = tok_count * topk, per_device * devices
    size = devices * cap
    pairs = [(routes_hbm, routes_ref), (gates_hbm, gates_ref), (tokens_hbm, tokens_ref), (cot_hbm, cot_ref)]
    copies = [pltpu.make_async_copy(source, target, sems.at[i]) for i, (source, target) in enumerate(pairs)]
    for copy in copies:
        copy.start()

    spread = (iota((tok_count, count), 1) // topk == iota((tok_count, count), 0)).astype(F32).astype(BF16)
    own = iota((topk, count), 1) % topk == iota((topk, count), 0)
    copies[0].wait()
    copies[1].wait()
    parts = [routes_ref[...].astype(F32).astype(BF16), *split3(gates_ref[...])]
    wide = [jnp.sum(jnp.where(own, dot(part, spread), 0.0), axis=0, keepdims=True) for part in parts]
    routes, gates = wide[0].astype(jnp.int32), (wide[1] + wide[2]) + wide[3]

    row = iota((experts, 1), 0)
    table = routes == (row % devices) * per_device + row // devices
    tok_table = dot(table.astype(F32).astype(BF16), spread, ((1,), (1,)))
    before = (iota((tok_count, tok_count), 0) < iota((tok_count, tok_count), 1)).astype(F32).astype(BF16)
    earlier = dot(tok_table.astype(BF16), before)
    tok_slot = jnp.where(tok_table > 0.5, earlier, -1.0).astype(jnp.int32)
    slots = jnp.where(table, (row * cap).astype(F32) + dot(earlier.astype(BF16), spread), 0.0)
    slot = jnp.sum(slots, axis=0, keepdims=True).astype(jnp.int32)

    mark = gates.astype(BF16).astype(F32)
    sums = jnp.sum(jnp.where(table, mark, 0.0), axis=1, keepdims=True)
    for j in range(per_device):
        sums_ref[:, j * 128 : (j + 1) * 128] = jnp.broadcast_to(sums[j * devices : (j + 1) * devices], (devices, 128))

    hits = tok_slot[:, None, :] == iota((experts, cap, tok_count), 1)
    picks_ref[...] = hits.astype(F32).reshape(experts * cap, tok_count).astype(BF16)
    step = 256
    copies[2].wait()
    copies[3].wait()
    outs = []
    for i in range(0, size, step):
        for j in range(per_device):
            rows = dot(picks_ref[j * size + i : j * size + i + step, :], tokens_ref[...])
            out_ref[i : i + step, j * model : (j + 1) * model] = rows.astype(BF16)
        for j in range(per_device):
            hit = slot == iota((step, 1), 0) + (j * size + i)
            gate = jnp.sum(jnp.where(hit, gates, 0.0), axis=1, keepdims=True)
            rows = dot(hit.astype(F32).astype(BF16), cot_ref[...])
            at = per_device * model + j * width
            out_ref[i : i + step, at : at + width] = (rows * gate).astype(BF16)
        part = pl.ds(i, step)
        outs.append(pltpu.make_async_copy(out_ref.at[part, :], out_hbm.at[part, :], sems.at[len(pairs) + len(outs)]))
        outs[-1].start()
    for copy in outs:
        copy.wait()


def grad_kernel(per_device, got_hbm, w_hbm, gp_hbm, gw_hbm, got_ref, w_ref, gp_ref, gw_ref, sems):
    size, hidden, model = gp_ref.shape[0], gp_ref.shape[1] // per_device, w_ref.shape[0]
    width = hidden // 2
    step, half = 256, 128
    tiles = size // step
    rows = [pl.ds(i * step, step) for i in range(tiles)]
    columns = [pl.ds(j * hidden, hidden) for j in range(per_device)]
    w_in = [
        pltpu.make_async_copy(w_hbm.at[:, columns[j]], w_ref.at[:, columns[j]], sems.at[j]) for j in range(per_device)
    ]
    got_in = [
        pltpu.make_async_copy(got_hbm.at[rows[i], :], got_ref.at[rows[i], :], sems.at[per_device + i])
        for i in range(tiles)
    ]
    for copy in (w_in[0], *got_in, *w_in[1:]):
        copy.start()
    outs = []
    for j in range(per_device):
        w_in[j].wait()
        at = j * hidden
        for i in range(0, size, half):
            if j == 0 and i % step == 0:
                got_in[i // step].wait()
            here = pl.ds(i, half)
            pre = dot(got_ref[here, j * model : (j + 1) * model], w_ref[:, columns[j]])
            gate, upper = pre[:, :width], pre[:, width:]
            sigma = jax.nn.sigmoid(gate)
            first = per_device * model + j * width
            common = got_ref[here, first : first + width].astype(F32) * sigma
            gp_ref[here, at : at + width] = (common * upper * (1.0 + gate * (1.0 - sigma))).astype(BF16)
            gp_ref[here, at + width : at + hidden] = (common * gate).astype(BF16)
        for i in range(0, model, step):
            part = got_ref[:, j * model + i : j * model + i + step]
            gw_ref[i : i + step, columns[j]] = dot(part, gp_ref[:, columns[j]], ((0,), (0,))).astype(BF16)
        for source, target in ((gp_ref, gp_hbm), (gw_ref, gw_hbm)):
            at = per_device + tiles + len(outs)
            outs.append(pltpu.make_async_copy(source.at[:, columns[j]], target.at[:, columns[j]], sems.at[at]))
            outs[-1].start()
    for copy in outs:
        copy.wait()


def route_kernel(gp_ref, w_ref, out_ref):
    step = 256
    for i in range(0, gp_ref.shape[0], step):
        out_ref[i : i + step, :] = dot(gp_ref[i : i + step, :], w_ref[...], ((1,), (1,))).astype(BF16)


def sum_kernel(per_device, picks_ref, back_ref, out_ref):
    tok_count, model = out_ref.shape
    size = back_ref.shape[0]
    total = jnp.zeros((tok_count, model), F32)
    for j in range(per_device):
        total += dot(picks_ref[j * size : (j + 1) * size, :], back_ref[:, j * model : (j + 1) * model], ((0,), (0,)))
    out_ref[...] = total.astype(BF16)


def call(kernel, outs, args, in_specs=None, out_specs=None, grid=(), scratch=(), flops=0, moved=0):
    whole = pl.BlockSpec(memory_space=pltpu.VMEM)
    return pl.pallas_call(
        kernel,
        grid=grid,
        out_shape=[jax.ShapeDtypeStruct(s, t) for s, t in outs],
        in_specs=in_specs or [whole] * len(args),
        out_specs=out_specs or [whole] * len(outs),
        scratch_shapes=scratch,
        compiler_params=pltpu.CompilerParams(vmem_limit_bytes=VMEM_LIMIT),
        cost_estimate=pl.CostEstimate(flops=flops, bytes_accessed=moved, transcendentals=0),
    )(*args)


def body(tokens, routes, route_gates, route_cotangent, gate_up):
    tok_count, topk = routes.shape
    width = route_cotangent.shape[2]
    model = tokens.shape[1]
    channels, per_device, hidden = gate_up.shape
    devices = lax.axis_size("expert")
    data_ways = lax.axis_size("dp")
    experts = per_device * devices
    cap = 3 * tok_count * topk // (2 * experts)
    size, count = devices * cap, tok_count * topk
    lanes = per_device * (model + width)
    vmem, hbm = pl.BlockSpec(memory_space=pltpu.VMEM), pl.BlockSpec(memory_space=pltpu.HBM)

    lift = 2.0**18
    sent = (gate_up.astype(F32) * lift).astype(jnp.float16).reshape(channels, per_device * hidden)

    packed, picks, sums = call(
        functools.partial(pack_kernel, per_device, devices, cap),
        [((size, lanes), BF16), ((per_device * size, tok_count), BF16), ((devices, per_device * 128), F32)],
        [routes.T, route_gates.T, tokens, route_cotangent.reshape(count, width)],
        in_specs=[hbm] * 4,
        out_specs=[hbm, vmem, vmem],
        scratch=[
            pltpu.VMEM((topk, tok_count), jnp.int32),
            pltpu.VMEM((topk, tok_count), F32),
            pltpu.VMEM((tok_count, model), BF16),
            pltpu.VMEM((count, width), BF16),
            pltpu.VMEM((size, lanes), BF16),
            pltpu.SemaphoreType.DMA((4 + size // 256,)),
        ],
        flops=2 * per_device * size * (tok_count * model + count * width),
        moved=2 * size * lanes,
    )
    sent, packed = lax.optimization_barrier((sent, packed))
    got = lax.all_to_all(packed, "expert", split_axis=0, concat_axis=0, tiled=True)
    gathered = lax.all_gather(sent, "dp", axis=0, tiled=True)
    full = (gathered.astype(F32) * (1.0 / lift)).astype(BF16)

    work = 2 * per_device * size * model * hidden
    grad_pre, part = call(
        functools.partial(grad_kernel, per_device),
        [((size, per_device * hidden), BF16), ((model, per_device * hidden), BF16)],
        [got, full],
        in_specs=[hbm, hbm],
        out_specs=[hbm, hbm],
        scratch=[
            pltpu.VMEM((size, lanes), BF16),
            pltpu.VMEM((model, per_device * hidden), BF16),
            pltpu.VMEM((size, per_device * hidden), BF16),
            pltpu.VMEM((model, per_device * hidden), BF16),
            pltpu.SemaphoreType.DMA((3 * per_device + size // 256,)),
        ],
        flops=2 * work,
        moved=12 * size * model,
    )
    mine = lax.psum_scatter(part, "dp", scatter_dimension=0, tiled=True)
    (back,) = call(
        route_kernel,
        [((size, per_device * model), BF16)],
        [grad_pre, full],
        in_specs=[pl.BlockSpec((size, hidden), lambda j: (0, j)), pl.BlockSpec((model, hidden), lambda j: (0, j))],
        out_specs=[pl.BlockSpec((size, model), lambda j: (0, j))],
        grid=(per_device,),
        flops=work,
        moved=12 * size * model,
    )
    returned = lax.all_to_all(back, "expert", split_axis=0, concat_axis=0, tiled=True)
    (grad_tokens,) = call(
        functools.partial(sum_kernel, per_device),
        [((tok_count, model), BF16)],
        [picks, returned],
        flops=2 * per_device * size * tok_count * model,
        moved=4 * size * model,
    )

    sums, _ = lax.optimization_barrier((sums, back))
    column = lax.psum(sums, "dp")
    column, _ = lax.optimization_barrier((column, returned))
    heard = lax.all_to_all(column, "expert", split_axis=0, concat_axis=0, tiled=True)
    totals = jnp.sum(heard, axis=0).reshape(per_device, 128)[:, 0]
    load = totals * (per_device / (tok_count * topk * data_ways))
    return (grad_tokens, mine.reshape(channels, per_device, hidden), load)


def solution(mesh):
    in_specs = (
        P(("dp", "expert"), None),
        P(("dp", "expert"), None),
        P(("dp", "expert"), None),
        P(("dp", "expert"), None, None),
        P("dp", "expert", None),
    )
    out_specs = (P(("dp", "expert"), None), P("dp", "expert", None), P("expert"))
    return jax.shard_map(body, mesh=mesh, in_specs=in_specs, out_specs=out_specs, check_vma=False)
```

```python
import functools

import jax
import jax.numpy as jnp
from jax import lax
from jax.experimental import pallas as pl
from jax.experimental.pallas import tpu as pltpu
from jax.sharding import PartitionSpec as P

F32 = jnp.float32
BF16 = jnp.bfloat16
VMEM_LIMIT = 60 * 1024 * 1024


def iota(shape, dim):
    return lax.broadcasted_iota(jnp.int32, shape, dim)


def dot(a, b, contract=((1,), (0,))):
    return lax.dot_general(a, b, (contract, ((), ())), preferred_element_type=F32)


def split3(x):
    high = x.astype(BF16)
    rest = x - high.astype(F32)
    middle = rest.astype(BF16)
    return high, middle, (rest - middle.astype(F32)).astype(BF16)


def pack_kernel(
    per_device, devices, cap, routes_hbm, gates_hbm, tokens_hbm, cot_hbm, out_hbm, picks_ref, routes_ref, gates_ref, tokens_ref, cot_ref, scaled_ref, out_ref, sems
):
    topk, tok_count = routes_ref.shape
    model, width = tokens_ref.shape[1], cot_ref.shape[1]
    count, experts = tok_count * topk, per_device * devices
    size = devices * cap
    pairs = [(routes_hbm, routes_ref), (gates_hbm, gates_ref), (tokens_hbm, tokens_ref), (cot_hbm, cot_ref)]
    copies = [pltpu.make_async_copy(source, target, sems.at[i]) for i, (source, target) in enumerate(pairs)]
    for copy in copies:
        copy.start()

    spread = (iota((tok_count, count), 1) // topk == iota((tok_count, count), 0)).astype(F32).astype(BF16)
    before = (iota((tok_count, tok_count), 0) < iota((tok_count, tok_count), 1)).astype(F32).astype(BF16)
    copies[0].wait()
    copies[1].wait()
    wide = dot(routes_ref[...].astype(F32).astype(BF16), spread)
    own = iota((topk, count), 1) % topk == iota((topk, count), 0)
    routes = jnp.sum(jnp.where(own, wide, 0.0), axis=0, keepdims=True).astype(jnp.int32)
    own = iota((count, topk), 0) % topk == iota((count, topk), 1)
    tall = sum(dot(spread, part, ((0,), (1,))) for part in split3(gates_ref[...]))
    gates = jnp.sum(jnp.where(own, tall, 0.0), axis=1, keepdims=True)

    row = iota((experts, 1), 0)
    table = routes == (row % devices) * per_device + row // devices
    flags = table.astype(F32).astype(BF16)
    tok_table = dot(flags, spread, ((1,), (1,)))
    earlier = dot(tok_table.astype(BF16), before)
    tok_slot = jnp.where(tok_table > 0.5, earlier, -1.0).astype(jnp.int32)
    slots = jnp.where(table, (row * cap).astype(F32) + dot(earlier.astype(BF16), spread), 0.0)
    slot = jnp.sum(slots, axis=0, keepdims=True).astype(jnp.int32)
    hits = tok_slot[:, None, :] == iota((experts, cap, tok_count), 1)
    picks_ref[...] = hits.astype(F32).reshape(experts * cap, tok_count).astype(BF16)

    mark = jnp.broadcast_to(gates, (count, 128)).astype(BF16)
    sums = dot(flags, mark)
    lane = iota((devices, 128), 1)
    notes = jnp.zeros((devices, 128), F32)
    for j in range(per_device):
        for p, part in enumerate(split3(sums[j * devices : (j + 1) * devices])):
            notes = jnp.where(lane == 3 * j + p, part.astype(F32), notes)
    notes = jnp.where(iota((devices, cap, 128), 1) == 0, notes[:, None, :], 0.0).reshape(size, 128).astype(BF16)

    step = 256
    copies[2].wait()
    copies[3].wait()
    scaled_ref[...] = (cot_ref[...].astype(F32) * gates).astype(BF16)
    first, last = per_device * model, per_device * (model + width)
    outs = []
    for i in range(0, size, step):
        for j in range(per_device):
            rows = dot(picks_ref[j * size + i : j * size + i + step, :], tokens_ref[...])
            out_ref[i : i + step, j * model : (j + 1) * model] = rows.astype(BF16)
        for j in range(per_device):
            hit = slot == iota((step, 1), 0) + (j * size + i)
            rows = dot(hit.astype(F32).astype(BF16), scaled_ref[...])
            out_ref[i : i + step, first + j * width : first + (j + 1) * width] = rows.astype(BF16)
        out_ref[i : i + step, last:] = notes[i : i + step]
        part = pl.ds(i, step)
        outs.append(pltpu.make_async_copy(out_ref.at[part, :], out_hbm.at[part, :], sems.at[len(pairs) + len(outs)]))
        outs[-1].start()
    for copy in outs:
        copy.wait()


def grad_kernel(per_device, got_hbm, w_hbm, gp_hbm, gw_hbm, got_ref, w_ref, gp_ref, gw_ref, sems):
    size, hidden, model = gp_ref.shape[0], gp_ref.shape[1] // per_device, w_ref.shape[0]
    width = hidden // 2
    step, half = 256, 128
    tiles = size // step
    rows = [pl.ds(i * step, step) for i in range(tiles)]
    columns = [pl.ds(j * hidden, hidden) for j in range(per_device)]
    w_in = [
        pltpu.make_async_copy(w_hbm.at[:, columns[j]], w_ref.at[:, columns[j]], sems.at[j]) for j in range(per_device)
    ]
    got_in = [
        pltpu.make_async_copy(got_hbm.at[rows[i], :], got_ref.at[rows[i], :], sems.at[per_device + i])
        for i in range(tiles)
    ]
    for copy in (w_in[0], *got_in, *w_in[1:]):
        copy.start()
    outs = []
    for j in range(per_device):
        w_in[j].wait()
        at = j * hidden
        for i in range(0, size, half):
            if j == 0 and i % step == 0:
                got_in[i // step].wait()
            here = pl.ds(i, half)
            pre = dot(got_ref[here, j * model : (j + 1) * model], w_ref[:, columns[j]])
            gate, upper = pre[:, :width], pre[:, width:]
            sigma = jax.nn.sigmoid(gate)
            first = per_device * model + j * width
            common = got_ref[here, first : first + width].astype(F32) * sigma
            gp_ref[here, at : at + width] = (common * upper * (1.0 + gate * (1.0 - sigma))).astype(BF16)
            gp_ref[here, at + width : at + hidden] = (common * gate).astype(BF16)
        for i in range(0, model, step):
            part = got_ref[:, j * model + i : j * model + i + step]
            gw_ref[i : i + step, columns[j]] = dot(part, gp_ref[:, columns[j]], ((0,), (0,))).astype(BF16)
        for source, target in ((gp_ref, gp_hbm), (gw_ref, gw_hbm)):
            at = per_device + tiles + len(outs)
            outs.append(pltpu.make_async_copy(source.at[:, columns[j]], target.at[:, columns[j]], sems.at[at]))
            outs[-1].start()
    for copy in outs:
        copy.wait()


def route_kernel(gp_ref, w_ref, out_ref):
    step = 256
    for i in range(0, gp_ref.shape[0], step):
        out_ref[i : i + step, :] = dot(gp_ref[i : i + step, :], w_ref[...], ((1,), (1,))).astype(BF16)


def sum_kernel(per_device, picks_ref, back_ref, out_ref):
    tok_count, model = out_ref.shape
    size = back_ref.shape[0]
    total = jnp.zeros((tok_count, model), F32)
    for j in range(per_device):
        total += dot(picks_ref[j * size : (j + 1) * size, :], back_ref[:, j * model : (j + 1) * model], ((0,), (0,)))
    out_ref[...] = total.astype(BF16)


def call(kernel, outs, args, in_specs=None, out_specs=None, grid=(), scratch=(), flops=0, moved=0):
    whole = pl.BlockSpec(memory_space=pltpu.VMEM)
    return pl.pallas_call(
        kernel,
        grid=grid,
        out_shape=[jax.ShapeDtypeStruct(s, t) for s, t in outs],
        in_specs=in_specs or [whole] * len(args),
        out_specs=out_specs or [whole] * len(outs),
        scratch_shapes=scratch,
        compiler_params=pltpu.CompilerParams(vmem_limit_bytes=VMEM_LIMIT),
        cost_estimate=pl.CostEstimate(flops=flops, bytes_accessed=moved, transcendentals=0),
    )(*args)


def body(tokens, routes, route_gates, route_cotangent, gate_up):
    tok_count, topk = routes.shape
    width = route_cotangent.shape[2]
    model = tokens.shape[1]
    channels, per_device, hidden = gate_up.shape
    devices = lax.axis_size("expert")
    data_ways = lax.axis_size("dp")
    experts = per_device * devices
    cap = 3 * tok_count * topk // (2 * experts)
    size, count = devices * cap, tok_count * topk
    lanes = per_device * (model + width) + 128
    vmem, hbm = pl.BlockSpec(memory_space=pltpu.VMEM), pl.BlockSpec(memory_space=pltpu.HBM)

    lift = 2.0**18
    sent = (gate_up.astype(F32) * lift).astype(jnp.float16).reshape(channels, per_device * hidden)

    packed, picks = call(
        functools.partial(pack_kernel, per_device, devices, cap),
        [((size, lanes), BF16), ((per_device * size, tok_count), BF16)],
        [routes.T, route_gates.T, tokens, route_cotangent.reshape(count, width)],
        in_specs=[hbm] * 4,
        out_specs=[hbm, vmem],
        scratch=[
            pltpu.VMEM((topk, tok_count), jnp.int32),
            pltpu.VMEM((topk, tok_count), F32),
            pltpu.VMEM((tok_count, model), BF16),
            pltpu.VMEM((count, width), BF16),
            pltpu.VMEM((count, width), BF16),
            pltpu.VMEM((size, lanes), BF16),
            pltpu.SemaphoreType.DMA((4 + size // 256,)),
        ],
        flops=2 * per_device * size * (tok_count * model + count * width),
        moved=2 * size * lanes,
    )
    got = lax.all_to_all(packed, "expert", split_axis=0, concat_axis=0, tiled=True)
    gathered = lax.all_gather(sent, "dp", axis=0, tiled=True)
    full = (gathered.astype(F32) * (1.0 / lift)).astype(BF16)

    work = 2 * per_device * size * model * hidden
    grad_pre, part = call(
        functools.partial(grad_kernel, per_device),
        [((size, per_device * hidden), BF16), ((model, per_device * hidden), BF16)],
        [got, full],
        in_specs=[hbm, hbm],
        out_specs=[hbm, hbm],
        scratch=[
            pltpu.VMEM((size, lanes), BF16),
            pltpu.VMEM((model, per_device * hidden), BF16),
            pltpu.VMEM((size, per_device * hidden), BF16),
            pltpu.VMEM((model, per_device * hidden), BF16),
            pltpu.SemaphoreType.DMA((3 * per_device + size // 256,)),
        ],
        flops=2 * work,
        moved=12 * size * model,
    )
    mine = lax.psum_scatter(part, "dp", scatter_dimension=0, tiled=True)
    (back,) = call(
        route_kernel,
        [((size, per_device * model), BF16)],
        [grad_pre, full],
        in_specs=[pl.BlockSpec((size, hidden), lambda j: (0, j)), pl.BlockSpec((model, hidden), lambda j: (0, j))],
        out_specs=[pl.BlockSpec((size, model), lambda j: (0, j))],
        grid=(per_device,),
        flops=work,
        moved=12 * size * model,
    )
    returned = lax.all_to_all(back, "expert", split_axis=0, concat_axis=0, tiled=True)
    (grad_tokens,) = call(
        functools.partial(sum_kernel, per_device),
        [((tok_count, model), BF16)],
        [picks, returned],
        flops=2 * per_device * size * tok_count * model,
        moved=4 * size * model,
    )

    notes, _ = lax.optimization_barrier((got[:, lanes - 128 :], back))
    plane = jnp.sum(notes.astype(F32), axis=0, keepdims=True)
    totals = lax.psum(plane, "dp")[0, : 3 * per_device].reshape(per_device, 3).sum(axis=1)
    load = totals * (per_device / (tok_count * topk * data_ways))
    return (grad_tokens, mine.reshape(channels, per_device, hidden), load)


def solution(mesh):
    in_specs = (
        P(("dp", "expert"), None),
        P(("dp", "expert"), None),
        P(("dp", "expert"), None),
        P(("dp", "expert"), None, None),
        P("dp", "expert", None),
    )
    out_specs = (P(("dp", "expert"), None), P("dp", "expert", None), P("expert"))
    return jax.shard_map(body, mesh=mesh, in_specs=in_specs, out_specs=out_specs, check_vma=False)
```

```python
import functools

import jax
import jax.numpy as jnp
from jax import lax
from jax.experimental import pallas as pl
from jax.experimental.pallas import tpu as pltpu
from jax.sharding import PartitionSpec as P

F32 = jnp.float32
BF16 = jnp.bfloat16
VMEM_LIMIT = 60 * 1024 * 1024


def iota(shape, dim):
    return lax.broadcasted_iota(jnp.int32, shape, dim)


def dot(a, b, contract=((1,), (0,))):
    return lax.dot_general(a, b, (contract, ((), ())), preferred_element_type=F32)


def split3(x):
    high = x.astype(BF16)
    rest = x - high.astype(F32)
    middle = rest.astype(BF16)
    return high, middle, (rest - middle.astype(F32)).astype(BF16)


def slots_of(routes, per_device, devices):
    topk, tok_count = routes.shape
    row = iota((per_device * devices, 1), 0)
    expert = (row % devices) * per_device + row // devices
    hit = jnp.zeros((per_device * devices, tok_count), F32)
    for k in range(topk):
        hit = jnp.where(routes[k : k + 1, :] == expert, 1.0, hit)
    before = (iota((tok_count, tok_count), 0) < iota((tok_count, tok_count), 1)).astype(F32).astype(BF16)
    return expert, dot(hit.astype(BF16), before), hit > 0.5


def picks_of(tok_slot, cap):
    experts, tok_count = tok_slot.shape
    hits = tok_slot[:, None, :] == iota((experts, cap, tok_count), 1)
    return hits.astype(F32).reshape(experts * cap, tok_count).astype(BF16)


def pack_kernel(
    per_device, devices, cap, routes_hbm, gates_hbm, tokens_hbm, cot_hbm, out_hbm, routes_ref, gates_ref, tokens_ref, cot_ref, scaled_ref, out_ref, sems
):
    topk, tok_count = routes_ref.shape
    model, width = tokens_ref.shape[1], cot_ref.shape[1]
    count, size = tok_count * topk, devices * cap
    pairs = [(routes_hbm, routes_ref), (gates_hbm, gates_ref), (tokens_hbm, tokens_ref), (cot_hbm, cot_ref)]
    copies = [pltpu.make_async_copy(source, target, sems.at[i]) for i, (source, target) in enumerate(pairs)]
    for copy in copies:
        copy.start()

    spread = (iota((tok_count, count), 1) // topk == iota((tok_count, count), 0)).astype(F32).astype(BF16)
    copies[0].wait()
    copies[1].wait()
    wide = dot(routes_ref[...].astype(F32).astype(BF16), spread)
    own = iota((topk, count), 1) % topk == iota((topk, count), 0)
    routes = jnp.sum(jnp.where(own, wide, 0.0), axis=0, keepdims=True).astype(jnp.int32)
    own = iota((count, topk), 0) % topk == iota((count, topk), 1)
    tall = sum(dot(spread, part, ((0,), (1,))) for part in split3(gates_ref[...]))
    gates = jnp.sum(jnp.where(own, tall, 0.0), axis=1, keepdims=True)

    expert, earlier, named = slots_of(routes_ref[...], per_device, devices)
    tok_slot = jnp.where(named, earlier, -1.0).astype(jnp.int32)
    row = iota((per_device * devices, 1), 0)
    slots = jnp.where(routes == expert, (row * cap).astype(F32) + dot(earlier.astype(BF16), spread), 0.0)
    slot = jnp.sum(slots, axis=0, keepdims=True).astype(jnp.int32)
    picks = picks_of(tok_slot, cap)

    step = 256
    copies[2].wait()
    copies[3].wait()
    scaled_ref[...] = (cot_ref[...].astype(F32) * gates).astype(BF16)
    first = per_device * model
    outs = []
    for i in range(0, size, step):
        for j in range(per_device):
            rows = dot(picks[j * size + i : j * size + i + step], tokens_ref[...])
            out_ref[i : i + step, j * model : (j + 1) * model] = rows.astype(BF16)
        for j in range(per_device):
            hit = slot == iota((step, 1), 0) + (j * size + i)
            rows = dot(hit.astype(F32).astype(BF16), scaled_ref[...])
            out_ref[i : i + step, first + j * width : first + (j + 1) * width] = rows.astype(BF16)
        part = pl.ds(i, step)
        outs.append(pltpu.make_async_copy(out_ref.at[part, :], out_hbm.at[part, :], sems.at[len(pairs) + len(outs)]))
        outs[-1].start()
    for copy in outs:
        copy.wait()


def tally_kernel(per_device, devices, cap, routes_ref, gates_ref, picks_ref, sums_ref):
    topk, tok_count = routes_ref.shape
    expert, earlier, named = slots_of(routes_ref[...], per_device, devices)
    picks_ref[...] = picks_of(jnp.where(named, earlier, -1.0).astype(jnp.int32), cap)
    mark = gates_ref[...].astype(BF16).astype(F32)
    sums = jnp.zeros((per_device * devices, 1), F32)
    for k in range(topk):
        chosen = jnp.where(routes_ref[k : k + 1, :] == expert, mark[k : k + 1, :], 0.0)
        sums += jnp.sum(chosen, axis=1, keepdims=True)
    row, lane = iota((per_device * devices, 128), 0), iota((per_device * devices, 128), 1)
    sums_ref[...] = jnp.sum(jnp.where(row == lane, sums, 0.0), axis=0, keepdims=True)


def grad_kernel(per_device, got_hbm, w_hbm, gp_hbm, gw_hbm, got_ref, w_ref, gp_ref, gw_ref, sems):
    size, hidden, model = gp_ref.shape[0], gp_ref.shape[1] // per_device, w_ref.shape[0]
    width = hidden // 2
    step, half = 256, 128
    tiles = size // step
    rows = [pl.ds(i * step, step) for i in range(tiles)]
    columns = [pl.ds(j * hidden, hidden) for j in range(per_device)]
    w_in = [
        pltpu.make_async_copy(w_hbm.at[:, columns[j]], w_ref.at[:, columns[j]], sems.at[j]) for j in range(per_device)
    ]
    got_in = [
        pltpu.make_async_copy(got_hbm.at[rows[i], :], got_ref.at[rows[i], :], sems.at[per_device + i])
        for i in range(tiles)
    ]
    for copy in (w_in[0], *got_in, *w_in[1:]):
        copy.start()
    outs = []
    for j in range(per_device):
        w_in[j].wait()
        at = j * hidden
        for i in range(0, size, half):
            if j == 0 and i % step == 0:
                got_in[i // step].wait()
            here = pl.ds(i, half)
            pre = dot(got_ref[here, j * model : (j + 1) * model], w_ref[:, columns[j]])
            gate, upper = pre[:, :width], pre[:, width:]
            sigma = jax.nn.sigmoid(gate)
            first = per_device * model + j * width
            common = got_ref[here, first : first + width].astype(F32) * sigma
            gp_ref[here, at : at + width] = (common * upper * (1.0 + gate * (1.0 - sigma))).astype(BF16)
            gp_ref[here, at + width : at + hidden] = (common * gate).astype(BF16)
        for i in range(0, model, step):
            part = got_ref[:, j * model + i : j * model + i + step]
            gw_ref[i : i + step, columns[j]] = dot(part, gp_ref[:, columns[j]], ((0,), (0,))).astype(BF16)
        for source, target in ((gp_ref, gp_hbm), (gw_ref, gw_hbm)):
            at = per_device + tiles + len(outs)
            outs.append(pltpu.make_async_copy(source.at[:, columns[j]], target.at[:, columns[j]], sems.at[at]))
            outs[-1].start()
    for copy in outs:
        copy.wait()


def route_kernel(gp_ref, w_ref, out_ref):
    step = 256
    for i in range(0, gp_ref.shape[0], step):
        out_ref[i : i + step, :] = dot(gp_ref[i : i + step, :], w_ref[...], ((1,), (1,))).astype(BF16)


def sum_kernel(per_device, picks_ref, back_ref, out_ref):
    tok_count, model = out_ref.shape
    size = back_ref.shape[0]
    total = jnp.zeros((tok_count, model), F32)
    for j in range(per_device):
        total += dot(picks_ref[j * size : (j + 1) * size, :], back_ref[:, j * model : (j + 1) * model], ((0,), (0,)))
    out_ref[...] = total.astype(BF16)


def call(kernel, outs, args, in_specs=None, out_specs=None, grid=(), scratch=(), flops=0, moved=0):
    whole = pl.BlockSpec(memory_space=pltpu.VMEM)
    return pl.pallas_call(
        kernel,
        grid=grid,
        out_shape=[jax.ShapeDtypeStruct(s, t) for s, t in outs],
        in_specs=in_specs or [whole] * len(args),
        out_specs=out_specs or [whole] * len(outs),
        scratch_shapes=scratch,
        compiler_params=pltpu.CompilerParams(vmem_limit_bytes=VMEM_LIMIT),
        cost_estimate=pl.CostEstimate(flops=flops, bytes_accessed=moved, transcendentals=0),
    )(*args)


def body(tokens, routes, route_gates, route_cotangent, gate_up):
    tok_count, topk = routes.shape
    width = route_cotangent.shape[2]
    model = tokens.shape[1]
    channels, per_device, hidden = gate_up.shape
    devices = lax.axis_size("expert")
    data_ways = lax.axis_size("dp")
    experts = per_device * devices
    cap = 3 * tok_count * topk // (2 * experts)
    size, count = devices * cap, tok_count * topk
    lanes = per_device * (model + width)
    vmem, hbm = pl.BlockSpec(memory_space=pltpu.VMEM), pl.BlockSpec(memory_space=pltpu.HBM)

    lift = 2.0**18
    sent = (gate_up.astype(F32) * lift).astype(jnp.float16).reshape(channels, per_device * hidden)

    (packed,) = call(
        functools.partial(pack_kernel, per_device, devices, cap),
        [((size, lanes), BF16)],
        [routes.T, route_gates.T, tokens, route_cotangent.reshape(count, width)],
        in_specs=[hbm] * 4,
        out_specs=[hbm],
        scratch=[
            pltpu.VMEM((topk, tok_count), jnp.int32),
            pltpu.VMEM((topk, tok_count), F32),
            pltpu.VMEM((tok_count, model), BF16),
            pltpu.VMEM((count, width), BF16),
            pltpu.VMEM((count, width), BF16),
            pltpu.VMEM((size, lanes), BF16),
            pltpu.SemaphoreType.DMA((4 + size // 256,)),
        ],
        flops=2 * per_device * size * (tok_count * model + count * width),
        moved=2 * size * lanes,
    )
    got = lax.all_to_all(packed, "expert", split_axis=0, concat_axis=0, tiled=True)
    gathered = lax.all_gather(sent, "dp", axis=0, tiled=True)
    full = (gathered.astype(F32) * (1.0 / lift)).astype(BF16)

    work = 2 * per_device * size * model * hidden
    grad_pre, part = call(
        functools.partial(grad_kernel, per_device),
        [((size, per_device * hidden), BF16), ((model, per_device * hidden), BF16)],
        [got, full],
        in_specs=[hbm, hbm],
        out_specs=[hbm, hbm],
        scratch=[
            pltpu.VMEM((size, lanes), BF16),
            pltpu.VMEM((model, per_device * hidden), BF16),
            pltpu.VMEM((size, per_device * hidden), BF16),
            pltpu.VMEM((model, per_device * hidden), BF16),
            pltpu.SemaphoreType.DMA((3 * per_device + size // 256,)),
        ],
        flops=2 * work,
        moved=12 * size * model,
    )
    mine = lax.psum_scatter(part, "dp", scatter_dimension=0, tiled=True)
    (back,) = call(
        route_kernel,
        [((size, per_device * model), BF16)],
        [grad_pre, full],
        in_specs=[pl.BlockSpec((size, hidden), lambda j: (0, j)), pl.BlockSpec((model, hidden), lambda j: (0, j))],
        out_specs=[pl.BlockSpec((size, model), lambda j: (0, j))],
        grid=(per_device,),
        flops=work,
        moved=12 * size * model,
    )
    later, _ = lax.optimization_barrier(((routes.T, route_gates.T), back))
    picks, sums = call(
        functools.partial(tally_kernel, per_device, devices, cap),
        [((per_device * size, tok_count), BF16), ((1, 128), F32)],
        later,
        moved=2 * per_device * size * tok_count,
    )
    returned = lax.all_to_all(back, "expert", split_axis=0, concat_axis=0, tiled=True)
    (grad_tokens,) = call(
        functools.partial(sum_kernel, per_device),
        [((tok_count, model), BF16)],
        [picks, returned],
        flops=2 * per_device * size * tok_count * model,
        moved=4 * size * model,
    )

    column = lax.psum(sums, "dp")[0, :experts].reshape(per_device, devices).T
    column = jnp.broadcast_to(column[:, :, None], (devices, per_device, 128)).reshape(devices, per_device * 128)
    column, _ = lax.optimization_barrier((column, returned))
    heard = lax.all_to_all(column, "expert", split_axis=0, concat_axis=0, tiled=True)
    totals = jnp.sum(heard, axis=0).reshape(per_device, 128)[:, 0]
    load = totals * (per_device / (tok_count * topk * data_ways))
    return (grad_tokens, mine.reshape(channels, per_device, hidden), load)


def solution(mesh):
    in_specs = (
        P(("dp", "expert"), None),
        P(("dp", "expert"), None),
        P(("dp", "expert"), None),
        P(("dp", "expert"), None, None),
        P("dp", "expert", None),
    )
    out_specs = (P(("dp", "expert"), None), P("dp", "expert", None), P("expert"))
    return jax.shard_map(body, mesh=mesh, in_specs=in_specs, out_specs=out_specs, check_vma=False)
```

```python
import functools

import jax
import jax.numpy as jnp
from jax import lax
from jax.experimental import pallas as pl
from jax.experimental.pallas import tpu as pltpu
from jax.sharding import PartitionSpec as P

F32 = jnp.float32
BF16 = jnp.bfloat16
VMEM_LIMIT = 60 * 1024 * 1024
ROOM = 32 * 1024 * 1024


def iota(shape, dim):
    return lax.broadcasted_iota(jnp.int32, shape, dim)


def dot(a, b, contract=((1,), (0,))):
    return lax.dot_general(a, b, (contract, ((), ())), preferred_element_type=F32)


def split3(x):
    high = x.astype(BF16)
    rest = x - high.astype(F32)
    middle = rest.astype(BF16)
    return high, middle, (rest - middle.astype(F32)).astype(BF16)


def slots_of(routes, per_device, devices):
    topk, tok_count = routes.shape
    row = iota((per_device * devices, 1), 0)
    expert = (row % devices) * per_device + row // devices
    hit = jnp.zeros((per_device * devices, tok_count), F32)
    for k in range(topk):
        hit = jnp.where(routes[k : k + 1, :] == expert, 1.0, hit)
    before = (iota((tok_count, tok_count), 0) < iota((tok_count, tok_count), 1)).astype(F32).astype(BF16)
    return expert, dot(hit.astype(BF16), before), hit > 0.5


def picks_of(tok_slot, cap):
    experts, tok_count = tok_slot.shape
    hits = tok_slot[:, None, :] == iota((experts, cap, tok_count), 1)
    return hits.astype(F32).reshape(experts * cap, tok_count).astype(BF16)


def pack_kernel(
    per_device, devices, cap, routes_hbm, gates_hbm, tokens_hbm, cot_hbm, out_hbm, routes_ref, gates_ref, tokens_ref, cot_ref, scaled_ref, out_ref, sems
):
    topk, tok_count = routes_ref.shape
    model, width = tokens_ref.shape[1], cot_ref.shape[1]
    count, size = tok_count * topk, devices * cap
    pairs = [(routes_hbm, routes_ref), (gates_hbm, gates_ref), (tokens_hbm, tokens_ref), (cot_hbm, cot_ref)]
    copies = [pltpu.make_async_copy(source, target, sems.at[i]) for i, (source, target) in enumerate(pairs)]
    for copy in copies:
        copy.start()

    spread = (iota((tok_count, count), 1) // topk == iota((tok_count, count), 0)).astype(F32).astype(BF16)
    copies[0].wait()
    copies[1].wait()
    wide = dot(routes_ref[...].astype(F32).astype(BF16), spread)
    own = iota((topk, count), 1) % topk == iota((topk, count), 0)
    routes = jnp.sum(jnp.where(own, wide, 0.0), axis=0, keepdims=True).astype(jnp.int32)
    own = iota((count, topk), 0) % topk == iota((count, topk), 1)
    tall = sum(dot(spread, part, ((0,), (1,))) for part in split3(gates_ref[...]))
    gates = jnp.sum(jnp.where(own, tall, 0.0), axis=1, keepdims=True)

    expert, earlier, named = slots_of(routes_ref[...], per_device, devices)
    tok_slot = jnp.where(named, earlier, -1.0).astype(jnp.int32)
    row = iota((per_device * devices, 1), 0)
    slots = jnp.where(routes == expert, (row * cap).astype(F32) + dot(earlier.astype(BF16), spread), 0.0)
    slot = jnp.sum(slots, axis=0, keepdims=True).astype(jnp.int32)
    picks = picks_of(tok_slot, cap)

    step = 256
    copies[2].wait()
    copies[3].wait()
    scaled_ref[...] = (cot_ref[...].astype(F32) * gates).astype(BF16)
    first = per_device * model
    outs = []

    def send(i, at, lanes):
        here = (pl.ds(i, step), pl.ds(at, lanes))
        outs.append(pltpu.make_async_copy(out_ref.at[here], out_hbm.at[here], sems.at[len(pairs) + len(outs)]))
        outs[-1].start()

    for i in range(0, size, step):
        for j in range(per_device):
            rows = dot(picks[j * size + i : j * size + i + step], tokens_ref[...])
            out_ref[i : i + step, j * model : (j + 1) * model] = rows.astype(BF16)
        send(i, 0, first)
        for j in range(per_device):
            hit = slot == iota((step, 1), 0) + (j * size + i)
            rows = dot(hit.astype(F32).astype(BF16), scaled_ref[...])
            out_ref[i : i + step, first + j * width : first + (j + 1) * width] = rows.astype(BF16)
        send(i, first, per_device * width)
    for copy in outs:
        copy.wait()


def tally_kernel(per_device, devices, cap, routes_ref, gates_ref, picks_ref, sums_ref):
    topk, tok_count = routes_ref.shape
    expert, earlier, named = slots_of(routes_ref[...], per_device, devices)
    picks_ref[...] = picks_of(jnp.where(named, earlier, -1.0).astype(jnp.int32), cap)
    mark = gates_ref[...].astype(BF16).astype(F32)
    sums = jnp.zeros((per_device * devices, 1), F32)
    for k in range(topk):
        chosen = jnp.where(routes_ref[k : k + 1, :] == expert, mark[k : k + 1, :], 0.0)
        sums += jnp.sum(chosen, axis=1, keepdims=True)
    row, lane = iota((per_device * devices, 128), 0), iota((per_device * devices, 128), 1)
    sums_ref[...] = jnp.sum(jnp.where(row == lane, sums, 0.0), axis=0, keepdims=True)


def starter(sems):
    copies = []

    def start(source, target):
        copies.append(pltpu.make_async_copy(source, target, sems.at[len(copies)]))
        copies[-1].start()
        return copies[-1]

    return start


def fetch_rows(start, got_hbm, got_ref, per_device, model, width, step):
    return [
        [
            start(got_hbm.at[pl.ds(i, step), pl.ds(at, count)], got_ref.at[pl.ds(i, step), pl.ds(at, count)])
            for at, count in ((j * model, model), (per_device * model + j * width, width))
        ]
        for j in range(per_device)
        for i in range(0, got_ref.shape[0], step)
    ]


def swiglu_grads(got_ref, w_ref, gp_ref, per_device, j, start, rows):
    model, hidden = w_ref.shape[0], w_ref.shape[1] // per_device
    width, here, at = hidden // 2, pl.ds(start, rows), j * hidden
    pre = dot(got_ref[here, j * model : (j + 1) * model], w_ref[:, at : at + hidden])
    gate, upper = pre[:, :width], pre[:, width:]
    sigma = jax.nn.sigmoid(gate)
    first = per_device * model + j * width
    common = got_ref[here, first : first + width].astype(F32) * sigma
    gp_ref[here, at : at + width] = (common * upper * (1.0 + gate * (1.0 - sigma))).astype(BF16)
    gp_ref[here, at + width : at + hidden] = (common * gate).astype(BF16)


def grad_kernel(per_device, got_hbm, w_ref, gw_hbm, got_ref, gp_ref, gw_ref, sems):
    model, hidden = w_ref.shape[0], w_ref.shape[1] // per_device
    size, step, half = got_ref.shape[0], 256, 128
    start = starter(sems)
    got_in = iter(fetch_rows(start, got_hbm, got_ref, per_device, model, hidden // 2, step))
    outs = []
    for j in range(per_device):
        at = j * hidden
        for i in range(0, size, half):
            if i % step == 0:
                for copy in next(got_in):
                    copy.wait()
            swiglu_grads(got_ref, w_ref, gp_ref, per_device, j, i, half)
        for i in range(0, model, step):
            part = got_ref[:, j * model + i : j * model + i + step]
            gw_ref[i : i + step, at : at + hidden] = dot(part, gp_ref[:, at : at + hidden], ((0,), (0,))).astype(BF16)
            here = (pl.ds(i, step), pl.ds(at, hidden))
            outs.append(start(gw_ref.at[here], gw_hbm.at[here]))
    for copy in outs:
        copy.wait()


def route_kernel(per_device, got_hbm, w_ref, back_hbm, got_ref, gp_ref, back_ref, sems):
    model, hidden = w_ref.shape[0], w_ref.shape[1] // per_device
    size, step = got_ref.shape[0], 256
    start = starter(sems)
    got_in = iter(fetch_rows(start, got_hbm, got_ref, per_device, model, hidden // 2, step))
    outs = []
    for j in range(per_device):
        at = j * hidden
        for i in range(0, size, step):
            for copy in next(got_in):
                copy.wait()
            for half in (0, step // 2):
                swiglu_grads(got_ref, w_ref, gp_ref, per_device, j, i + half, step // 2)
            here = (pl.ds(i, step), pl.ds(j * model, model))
            rows = dot(gp_ref[i : i + step, at : at + hidden], w_ref[:, at : at + hidden], ((1,), (1,)))
            back_ref[i : i + step, j * model : (j + 1) * model] = rows.astype(BF16)
            outs.append(start(back_ref.at[here], back_hbm.at[here]))
    for copy in outs:
        copy.wait()


def sum_kernel(per_device, picks_ref, back_ref, out_ref):
    tok_count, model = out_ref.shape
    size = back_ref.shape[0]
    total = jnp.zeros((tok_count, model), F32)
    for j in range(per_device):
        total += dot(picks_ref[j * size : (j + 1) * size, :], back_ref[:, j * model : (j + 1) * model], ((0,), (0,)))
    out_ref[...] = total.astype(BF16)


def call(kernel, outs, args, in_specs=None, out_specs=None, grid=(), scratch=(), flops=0, moved=0, room=VMEM_LIMIT):
    whole = pl.BlockSpec(memory_space=pltpu.VMEM)
    return pl.pallas_call(
        kernel,
        grid=grid,
        out_shape=[jax.ShapeDtypeStruct(s, t) for s, t in outs],
        in_specs=in_specs or [whole] * len(args),
        out_specs=out_specs or [whole] * len(outs),
        scratch_shapes=scratch,
        compiler_params=pltpu.CompilerParams(vmem_limit_bytes=room),
        cost_estimate=pl.CostEstimate(flops=flops, bytes_accessed=moved, transcendentals=0),
    )(*args)


def body(tokens, routes, route_gates, route_cotangent, gate_up):
    tok_count, topk = routes.shape
    width = route_cotangent.shape[2]
    model = tokens.shape[1]
    channels, per_device, hidden = gate_up.shape
    devices = lax.axis_size("expert")
    data_ways = lax.axis_size("dp")
    experts = per_device * devices
    cap = 3 * tok_count * topk // (2 * experts)
    size, count = devices * cap, tok_count * topk
    lanes = per_device * (model + width)
    vmem, hbm = pl.BlockSpec(memory_space=pltpu.VMEM), pl.BlockSpec(memory_space=pltpu.HBM)

    lift = 2.0**18
    sent = (gate_up.astype(F32) * lift).astype(jnp.float16).reshape(channels, per_device * hidden)

    (packed,) = call(
        functools.partial(pack_kernel, per_device, devices, cap),
        [((size, lanes), BF16)],
        [routes.T, route_gates.T, tokens, route_cotangent.reshape(count, width)],
        in_specs=[hbm] * 4,
        out_specs=[hbm],
        scratch=[
            pltpu.VMEM((topk, tok_count), jnp.int32),
            pltpu.VMEM((topk, tok_count), F32),
            pltpu.VMEM((tok_count, model), BF16),
            pltpu.VMEM((count, width), BF16),
            pltpu.VMEM((count, width), BF16),
            pltpu.VMEM((size, lanes), BF16),
            pltpu.SemaphoreType.DMA((4 + 2 * (size // 256),)),
        ],
        flops=2 * per_device * size * (tok_count * model + count * width),
        moved=2 * size * lanes,
    )
    got = lax.all_to_all(packed, "expert", split_axis=0, concat_axis=0, tiled=True)
    gathered = lax.all_gather(sent, "dp", axis=0, tiled=True)
    full = (gathered.astype(F32) * (1.0 / lift)).astype(BF16)

    work = 2 * per_device * size * model * hidden
    tiles = size // 256
    held = [pltpu.VMEM((size, lanes), BF16), pltpu.VMEM((size, per_device * hidden), BF16)]
    (part,) = call(
        functools.partial(grad_kernel, per_device),
        [((model, per_device * hidden), BF16)],
        [got, full],
        in_specs=[hbm, vmem],
        out_specs=[hbm],
        scratch=[
            *held,
            pltpu.VMEM((model, per_device * hidden), BF16),
            pltpu.SemaphoreType.DMA((per_device * (2 * tiles + model // 256),)),
        ],
        flops=2 * work,
        moved=12 * size * model,
        room=ROOM,
    )
    mine = lax.psum_scatter(part, "dp", scatter_dimension=0, tiled=True)
    (back,) = call(
        functools.partial(route_kernel, per_device),
        [((size, per_device * model), BF16)],
        [got, full],
        in_specs=[hbm, vmem],
        out_specs=[hbm],
        scratch=[*held, pltpu.VMEM((size, per_device * model), BF16), pltpu.SemaphoreType.DMA((3 * per_device * tiles,))],
        flops=2 * work,
        moved=12 * size * model,
        room=ROOM,
    )
    later, _ = lax.optimization_barrier(((routes.T, route_gates.T), back))
    picks, sums = call(
        functools.partial(tally_kernel, per_device, devices, cap),
        [((per_device * size, tok_count), BF16), ((1, 128), F32)],
        later,
        moved=2 * per_device * size * tok_count,
    )
    returned = lax.all_to_all(back, "expert", split_axis=0, concat_axis=0, tiled=True)
    (grad_tokens,) = call(
        functools.partial(sum_kernel, per_device),
        [((tok_count, model), BF16)],
        [picks, returned],
        flops=2 * per_device * size * tok_count * model,
        moved=4 * size * model,
    )

    column = lax.psum(sums, "dp")[0, :experts].reshape(per_device, devices).T
    column = jnp.broadcast_to(column[:, :, None], (devices, per_device, 128)).reshape(devices, per_device * 128)
    column, _ = lax.optimization_barrier((column, returned))
    heard = lax.all_to_all(column, "expert", split_axis=0, concat_axis=0, tiled=True)
    totals = jnp.sum(heard, axis=0).reshape(per_device, 128)[:, 0]
    load = totals * (per_device / (tok_count * topk * data_ways))
    return (grad_tokens, mine.reshape(channels, per_device, hidden), load)


def solution(mesh):
    in_specs = (
        P(("dp", "expert"), None),
        P(("dp", "expert"), None),
        P(("dp", "expert"), None),
        P(("dp", "expert"), None, None),
        P("dp", "expert", None),
    )
    out_specs = (P(("dp", "expert"), None), P("dp", "expert", None), P("expert"))
    return jax.shard_map(body, mesh=mesh, in_specs=in_specs, out_specs=out_specs, check_vma=False)
```

```python
import functools

import jax
import jax.numpy as jnp
from jax import lax
from jax.experimental import pallas as pl
from jax.experimental.pallas import tpu as pltpu
from jax.sharding import PartitionSpec as P

F32 = jnp.float32
BF16 = jnp.bfloat16
VMEM_LIMIT = 60 * 1024 * 1024
ROOM = 32 * 1024 * 1024


def iota(shape, dim):
    return lax.broadcasted_iota(jnp.int32, shape, dim)


def dot(a, b, contract=((1,), (0,))):
    return lax.dot_general(a, b, (contract, ((), ())), preferred_element_type=F32)


def split3(x):
    high = x.astype(BF16)
    rest = x - high.astype(F32)
    middle = rest.astype(BF16)
    return high, middle, (rest - middle.astype(F32)).astype(BF16)


def slots_of(routes, per_device, devices):
    topk, tok_count = routes.shape
    row = iota((per_device * devices, 1), 0)
    expert = (row % devices) * per_device + row // devices
    hit = jnp.zeros((per_device * devices, tok_count), F32)
    for k in range(topk):
        hit = jnp.where(routes[k : k + 1, :] == expert, 1.0, hit)
    before = (iota((tok_count, tok_count), 0) < iota((tok_count, tok_count), 1)).astype(F32).astype(BF16)
    return expert, dot(hit.astype(BF16), before), hit > 0.5


def picks_of(tok_slot, cap):
    experts, tok_count = tok_slot.shape
    hits = tok_slot[:, None, :] == iota((experts, cap, tok_count), 1)
    return hits.astype(F32).reshape(experts * cap, tok_count).astype(BF16)


def pack_kernel(
    per_device, devices, cap, routes_hbm, gates_hbm, tokens_hbm, cot_hbm, out_hbm, routes_ref, gates_ref, tokens_ref, cot_ref, scaled_ref, out_ref, sems
):
    topk, tok_count = routes_ref.shape
    model, width = tokens_ref.shape[1], cot_ref.shape[1]
    count, size = tok_count * topk, devices * cap
    pairs = [(routes_hbm, routes_ref), (gates_hbm, gates_ref), (tokens_hbm, tokens_ref), (cot_hbm, cot_ref)]
    copies = [pltpu.make_async_copy(source, target, sems.at[i]) for i, (source, target) in enumerate(pairs)]
    for copy in copies:
        copy.start()

    spread = (iota((tok_count, count), 1) // topk == iota((tok_count, count), 0)).astype(F32).astype(BF16)
    copies[0].wait()
    copies[1].wait()
    wide = dot(routes_ref[...].astype(F32).astype(BF16), spread)
    own = iota((topk, count), 1) % topk == iota((topk, count), 0)
    routes = jnp.sum(jnp.where(own, wide, 0.0), axis=0, keepdims=True).astype(jnp.int32)
    own = iota((count, topk), 0) % topk == iota((count, topk), 1)
    tall = sum(dot(spread, part, ((0,), (1,))) for part in split3(gates_ref[...]))
    gates = jnp.sum(jnp.where(own, tall, 0.0), axis=1, keepdims=True)

    expert, earlier, named = slots_of(routes_ref[...], per_device, devices)
    tok_slot = jnp.where(named, earlier, -1.0).astype(jnp.int32)
    row = iota((per_device * devices, 1), 0)
    slots = jnp.where(routes == expert, (row * cap).astype(F32) + dot(earlier.astype(BF16), spread), 0.0)
    slot = jnp.sum(slots, axis=0, keepdims=True).astype(jnp.int32)
    picks = picks_of(tok_slot, cap)

    step = 256
    copies[2].wait()
    copies[3].wait()
    scaled_ref[...] = (cot_ref[...].astype(F32) * gates).astype(BF16)
    first = per_device * model
    outs = []

    def send(i, at, lanes):
        here = (pl.ds(i, step), pl.ds(at, lanes))
        outs.append(pltpu.make_async_copy(out_ref.at[here], out_hbm.at[here], sems.at[len(pairs) + len(outs)]))
        outs[-1].start()

    for i in range(0, size, step):
        for j in range(per_device):
            rows = dot(picks[j * size + i : j * size + i + step], tokens_ref[...])
            out_ref[i : i + step, j * model : (j + 1) * model] = rows.astype(BF16)
        send(i, 0, first)
        for j in range(per_device):
            hit = slot == iota((step, 1), 0) + (j * size + i)
            rows = dot(hit.astype(F32).astype(BF16), scaled_ref[...])
            out_ref[i : i + step, first + j * width : first + (j + 1) * width] = rows.astype(BF16)
        send(i, first, per_device * width)
    for copy in outs:
        copy.wait()


def tally_kernel(per_device, devices, cap, routes_ref, gates_ref, picks_ref, sums_ref):
    topk, tok_count = routes_ref.shape
    expert, earlier, named = slots_of(routes_ref[...], per_device, devices)
    picks_ref[...] = picks_of(jnp.where(named, earlier, -1.0).astype(jnp.int32), cap)
    mark = gates_ref[...].astype(BF16).astype(F32)
    sums = jnp.zeros((per_device * devices, 1), F32)
    for k in range(topk):
        chosen = jnp.where(routes_ref[k : k + 1, :] == expert, mark[k : k + 1, :], 0.0)
        sums += jnp.sum(chosen, axis=1, keepdims=True)
    row, lane = iota((per_device * devices, 128), 0), iota((per_device * devices, 128), 1)
    sums_ref[...] = jnp.sum(jnp.where(row == lane, sums, 0.0), axis=0, keepdims=True)


def starter(sems):
    copies = []

    def start(source, target):
        copies.append(pltpu.make_async_copy(source, target, sems.at[len(copies)]))
        copies[-1].start()
        return copies[-1]

    return start


def fetch_rows(start, got_hbm, got_ref, per_device, model, width, step):
    return [
        [
            start(got_hbm.at[pl.ds(i, step), pl.ds(at, count)], got_ref.at[pl.ds(i, step), pl.ds(at, count)])
            for at, count in ((j * model, model), (per_device * model + j * width, width))
        ]
        for j in range(per_device)
        for i in range(0, got_ref.shape[0], step)
    ]


def swiglu_grads(got_ref, w_ref, gp_ref, per_device, j, start, rows):
    model, hidden = w_ref.shape[0], w_ref.shape[1] // per_device
    width, here, at = hidden // 2, pl.ds(start, rows), j * hidden
    pre = dot(got_ref[here, j * model : (j + 1) * model], w_ref[:, at : at + hidden])
    gate, upper = pre[:, :width], pre[:, width:]
    sigma = jax.nn.sigmoid(gate)
    first = per_device * model + j * width
    common = got_ref[here, first : first + width].astype(F32) * sigma
    gp_ref[here, at : at + width] = (common * upper * (1.0 + gate * (1.0 - sigma))).astype(BF16)
    gp_ref[here, at + width : at + hidden] = (common * gate).astype(BF16)


def grad_kernel(per_device, got_hbm, w_ref, gw_hbm, got_ref, gp_ref, gw_ref, sems):
    model, hidden = w_ref.shape[0], w_ref.shape[1] // per_device
    size, step, half = got_ref.shape[0], 256, 128
    start = starter(sems)
    got_in = iter(fetch_rows(start, got_hbm, got_ref, per_device, model, hidden // 2, step))
    outs = []
    for j in range(per_device):
        at = j * hidden
        for i in range(0, size, half):
            if i % step == 0:
                for copy in next(got_in):
                    copy.wait()
            swiglu_grads(got_ref, w_ref, gp_ref, per_device, j, i, half)
        for i in range(0, model, step):
            part = got_ref[:, j * model + i : j * model + i + step]
            gw_ref[i : i + step, at : at + hidden] = dot(part, gp_ref[:, at : at + hidden], ((0,), (0,))).astype(BF16)
            here = (pl.ds(i, step), pl.ds(at, hidden))
            outs.append(start(gw_ref.at[here], gw_hbm.at[here]))
    for copy in outs:
        copy.wait()


def route_kernel(per_device, got_hbm, w_ref, back_hbm, got_ref, gp_ref, back_ref, sems):
    model, hidden = w_ref.shape[0], w_ref.shape[1] // per_device
    size, step = got_ref.shape[0], 256
    start = starter(sems)
    got_in = iter(fetch_rows(start, got_hbm, got_ref, per_device, model, hidden // 2, step))
    outs = []
    for j in range(per_device):
        at = j * hidden
        for i in range(0, size, step):
            for copy in next(got_in):
                copy.wait()
            for half in (0, step // 2):
                swiglu_grads(got_ref, w_ref, gp_ref, per_device, j, i + half, step // 2)
            here = (pl.ds(i, step), pl.ds(j * model, model))
            rows = dot(gp_ref[i : i + step, at : at + hidden], w_ref[:, at : at + hidden], ((1,), (1,)))
            back_ref[i : i + step, j * model : (j + 1) * model] = rows.astype(BF16)
            outs.append(start(back_ref.at[here], back_hbm.at[here]))
    for copy in outs:
        copy.wait()


def sum_kernel(per_device, picks_ref, back_ref, out_ref):
    tok_count, model = out_ref.shape
    size = back_ref.shape[0]
    total = jnp.zeros((tok_count, model), F32)
    for j in range(per_device):
        total += dot(picks_ref[j * size : (j + 1) * size, :], back_ref[:, j * model : (j + 1) * model], ((0,), (0,)))
    out_ref[...] = total.astype(BF16)


STEPS = tuple(2.0 ** (-10 * k) for k in range(1, 11))
NOTE_ROWS = 8


def to_half(weights):
    wide = weights.astype(F32)
    top = jnp.max(jnp.abs(wide))
    level, lift = jnp.float32(0.0), jnp.float32(2.0**15)
    for bound in STEPS:
        level += jnp.where(top < bound, 1.0, 0.0)
        lift *= jnp.where(top < bound, 2.0**10, 1.0)
    note = jnp.broadcast_to(level, (NOTE_ROWS, weights.shape[1]))
    return jnp.concatenate([wide * lift, note], axis=0).astype(jnp.float16)


def from_half(gathered, shards):
    parts = gathered.reshape(shards, -1, gathered.shape[1])
    level = parts[:, -1, 0].astype(F32)
    drop = jnp.full((shards,), 2.0**-15, F32)
    for k in range(len(STEPS)):
        drop *= jnp.where(level > k + 0.5, 2.0**-10, 1.0)
    whole = parts[:, :-NOTE_ROWS].astype(F32) * drop[:, None, None]
    return whole.astype(BF16).reshape(-1, gathered.shape[1])


def call(kernel, outs, args, in_specs=None, out_specs=None, grid=(), scratch=(), flops=0, moved=0, room=VMEM_LIMIT):
    whole = pl.BlockSpec(memory_space=pltpu.VMEM)
    return pl.pallas_call(
        kernel,
        grid=grid,
        out_shape=[jax.ShapeDtypeStruct(s, t) for s, t in outs],
        in_specs=in_specs or [whole] * len(args),
        out_specs=out_specs or [whole] * len(outs),
        scratch_shapes=scratch,
        compiler_params=pltpu.CompilerParams(vmem_limit_bytes=room),
        cost_estimate=pl.CostEstimate(flops=flops, bytes_accessed=moved, transcendentals=0),
    )(*args)


def body(tokens, routes, route_gates, route_cotangent, gate_up):
    tok_count, topk = routes.shape
    width = route_cotangent.shape[2]
    model = tokens.shape[1]
    channels, per_device, hidden = gate_up.shape
    devices = lax.axis_size("expert")
    data_ways = lax.axis_size("dp")
    experts = per_device * devices
    cap = 3 * tok_count * topk // (2 * experts)
    size, count = devices * cap, tok_count * topk
    lanes = per_device * (model + width)
    vmem, hbm = pl.BlockSpec(memory_space=pltpu.VMEM), pl.BlockSpec(memory_space=pltpu.HBM)

    (packed,) = call(
        functools.partial(pack_kernel, per_device, devices, cap),
        [((size, lanes), BF16)],
        [routes.T, route_gates.T, tokens, route_cotangent.reshape(count, width)],
        in_specs=[hbm] * 4,
        out_specs=[hbm],
        scratch=[
            pltpu.VMEM((topk, tok_count), jnp.int32),
            pltpu.VMEM((topk, tok_count), F32),
            pltpu.VMEM((tok_count, model), BF16),
            pltpu.VMEM((count, width), BF16),
            pltpu.VMEM((count, width), BF16),
            pltpu.VMEM((size, lanes), BF16),
            pltpu.SemaphoreType.DMA((4 + 2 * (size // 256),)),
        ],
        flops=2 * per_device * size * (tok_count * model + count * width),
        moved=2 * size * lanes,
    )
    got = lax.all_to_all(packed, "expert", split_axis=0, concat_axis=0, tiled=True)
    later, _ = lax.optimization_barrier((gate_up, packed))
    sent = to_half(later.reshape(channels, per_device * hidden))
    full = from_half(lax.all_gather(sent, "dp", axis=0, tiled=True), data_ways)

    work = 2 * per_device * size * model * hidden
    tiles = size // 256
    held = [pltpu.VMEM((size, lanes), BF16), pltpu.VMEM((size, per_device * hidden), BF16)]
    (part,) = call(
        functools.partial(grad_kernel, per_device),
        [((model, per_device * hidden), BF16)],
        [got, full],
        in_specs=[hbm, vmem],
        out_specs=[hbm],
        scratch=[
            *held,
            pltpu.VMEM((model, per_device * hidden), BF16),
            pltpu.SemaphoreType.DMA((per_device * (2 * tiles + model // 256),)),
        ],
        flops=2 * work,
        moved=12 * size * model,
        room=ROOM,
    )
    mine = lax.psum_scatter(part, "dp", scatter_dimension=0, tiled=True)
    (back,) = call(
        functools.partial(route_kernel, per_device),
        [((size, per_device * model), BF16)],
        [got, full],
        in_specs=[hbm, vmem],
        out_specs=[hbm],
        scratch=[*held, pltpu.VMEM((size, per_device * model), BF16), pltpu.SemaphoreType.DMA((3 * per_device * tiles,))],
        flops=2 * work,
        moved=12 * size * model,
        room=ROOM,
    )
    later, _ = lax.optimization_barrier(((routes.T, route_gates.T), back))
    picks, sums = call(
        functools.partial(tally_kernel, per_device, devices, cap),
        [((per_device * size, tok_count), BF16), ((1, 128), F32)],
        later,
        moved=2 * per_device * size * tok_count,
    )
    returned = lax.all_to_all(back, "expert", split_axis=0, concat_axis=0, tiled=True)
    (grad_tokens,) = call(
        functools.partial(sum_kernel, per_device),
        [((tok_count, model), BF16)],
        [picks, returned],
        flops=2 * per_device * size * tok_count * model,
        moved=4 * size * model,
    )

    column = lax.psum(sums, "dp")[0, :experts].reshape(per_device, devices).T
    column = jnp.broadcast_to(column[:, :, None], (devices, per_device, 128)).reshape(devices, per_device * 128)
    column, _ = lax.optimization_barrier((column, returned))
    heard = lax.all_to_all(column, "expert", split_axis=0, concat_axis=0, tiled=True)
    totals = jnp.sum(heard, axis=0).reshape(per_device, 128)[:, 0]
    load = totals * (per_device / (tok_count * topk * data_ways))
    return (grad_tokens, mine.reshape(channels, per_device, hidden), load)


def solution(mesh):
    in_specs = (
        P(("dp", "expert"), None),
        P(("dp", "expert"), None),
        P(("dp", "expert"), None),
        P(("dp", "expert"), None, None),
        P("dp", "expert", None),
    )
    out_specs = (P(("dp", "expert"), None), P("dp", "expert", None), P("expert"))
    return jax.shard_map(body, mesh=mesh, in_specs=in_specs, out_specs=out_specs, check_vma=False)
```

```python
import functools

import jax
import jax.numpy as jnp
from jax import lax
from jax.experimental import pallas as pl
from jax.experimental.pallas import tpu as pltpu
from jax.sharding import PartitionSpec as P

F32 = jnp.float32
BF16 = jnp.bfloat16
VMEM_LIMIT = 60 * 1024 * 1024
ROOM = 32 * 1024 * 1024


def iota(shape, dim):
    return lax.broadcasted_iota(jnp.int32, shape, dim)


def dot(a, b, contract=((1,), (0,))):
    return lax.dot_general(a, b, (contract, ((), ())), preferred_element_type=F32)


def split3(x):
    high = x.astype(BF16)
    rest = x - high.astype(F32)
    middle = rest.astype(BF16)
    return high, middle, (rest - middle.astype(F32)).astype(BF16)


def slots_of(routes, per_device, devices):
    topk, tok_count = routes.shape
    row = iota((per_device * devices, 1), 0)
    expert = (row % devices) * per_device + row // devices
    hit = jnp.zeros((per_device * devices, tok_count), F32)
    for k in range(topk):
        hit = jnp.where(routes[k : k + 1, :] == expert, 1.0, hit)
    before = (iota((tok_count, tok_count), 0) < iota((tok_count, tok_count), 1)).astype(F32).astype(BF16)
    return expert, dot(hit.astype(BF16), before), hit > 0.5


def picks_of(tok_slot, cap):
    experts, tok_count = tok_slot.shape
    hits = tok_slot[:, None, :] == iota((experts, cap, tok_count), 1)
    return hits.astype(F32).reshape(experts * cap, tok_count).astype(BF16)


def pack_kernel(
    per_device, devices, cap, routes_hbm, gates_hbm, tokens_hbm, cot_hbm, out_hbm, routes_ref, gates_ref, tokens_ref, cot_ref, scaled_ref, out_ref, sems
):
    topk, tok_count = routes_ref.shape
    model, width = tokens_ref.shape[1], cot_ref.shape[1]
    count, size = tok_count * topk, devices * cap
    pairs = [(routes_hbm, routes_ref), (gates_hbm, gates_ref), (tokens_hbm, tokens_ref), (cot_hbm, cot_ref)]
    copies = [pltpu.make_async_copy(source, target, sems.at[i]) for i, (source, target) in enumerate(pairs)]
    for copy in copies:
        copy.start()

    spread = (iota((tok_count, count), 1) // topk == iota((tok_count, count), 0)).astype(F32).astype(BF16)
    copies[0].wait()
    copies[1].wait()
    wide = dot(routes_ref[...].astype(F32).astype(BF16), spread)
    own = iota((topk, count), 1) % topk == iota((topk, count), 0)
    routes = jnp.sum(jnp.where(own, wide, 0.0), axis=0, keepdims=True).astype(jnp.int32)
    own = iota((count, topk), 0) % topk == iota((count, topk), 1)
    tall = sum(dot(spread, part, ((0,), (1,))) for part in split3(gates_ref[...]))
    gates = jnp.sum(jnp.where(own, tall, 0.0), axis=1, keepdims=True)

    expert, earlier, named = slots_of(routes_ref[...], per_device, devices)
    tok_slot = jnp.where(named, earlier, -1.0).astype(jnp.int32)
    row = iota((per_device * devices, 1), 0)
    slots = jnp.where(routes == expert, (row * cap).astype(F32) + dot(earlier.astype(BF16), spread), 0.0)
    slot = jnp.sum(slots, axis=0, keepdims=True).astype(jnp.int32)
    picks = picks_of(tok_slot, cap)

    step = 256
    copies[2].wait()
    copies[3].wait()
    scaled_ref[...] = (cot_ref[...].astype(F32) * gates).astype(BF16)
    first = per_device * model
    outs = []

    def send(i, at, lanes):
        here = (pl.ds(i, step), pl.ds(at, lanes))
        outs.append(pltpu.make_async_copy(out_ref.at[here], out_hbm.at[here], sems.at[len(pairs) + len(outs)]))
        outs[-1].start()

    for i in range(0, size, step):
        for j in range(per_device):
            rows = dot(picks[j * size + i : j * size + i + step], tokens_ref[...])
            out_ref[i : i + step, j * model : (j + 1) * model] = rows.astype(BF16)
        send(i, 0, first)
        for j in range(per_device):
            hit = slot == iota((step, 1), 0) + (j * size + i)
            rows = dot(hit.astype(F32).astype(BF16), scaled_ref[...])
            out_ref[i : i + step, first + j * width : first + (j + 1) * width] = rows.astype(BF16)
        send(i, first, per_device * width)
    for copy in outs:
        copy.wait()


def tally_kernel(per_device, devices, cap, routes_ref, gates_ref, picks_ref, sums_ref):
    topk, tok_count = routes_ref.shape
    expert, earlier, named = slots_of(routes_ref[...], per_device, devices)
    picks_ref[...] = picks_of(jnp.where(named, earlier, -1.0).astype(jnp.int32), cap)
    mark = gates_ref[...].astype(BF16).astype(F32)
    sums = jnp.zeros((per_device * devices, 1), F32)
    for k in range(topk):
        chosen = jnp.where(routes_ref[k : k + 1, :] == expert, mark[k : k + 1, :], 0.0)
        sums += jnp.sum(chosen, axis=1, keepdims=True)
    row, lane = iota((per_device * devices, 128), 0), iota((per_device * devices, 128), 1)
    sums_ref[...] = jnp.sum(jnp.where(row == lane, sums, 0.0), axis=0, keepdims=True)


def starter(sems):
    copies = []

    def start(source, target):
        copies.append(pltpu.make_async_copy(source, target, sems.at[len(copies)]))
        copies[-1].start()
        return copies[-1]

    return start


def fetch_rows(start, got_hbm, got_ref, per_device, model, width, step):
    return [
        [
            start(got_hbm.at[pl.ds(i, step), pl.ds(at, count)], got_ref.at[pl.ds(i, step), pl.ds(at, count)])
            for at, count in ((j * model, model), (per_device * model + j * width, width))
        ]
        for j in range(per_device)
        for i in range(0, got_ref.shape[0], step)
    ]


def swiglu_grads(got_ref, w_ref, gp_ref, per_device, j, start, rows):
    model, hidden = w_ref.shape[0], w_ref.shape[1] // per_device
    width, here, at = hidden // 2, pl.ds(start, rows), j * hidden
    pre = dot(got_ref[here, j * model : (j + 1) * model], w_ref[:, at : at + hidden])
    gate, upper = pre[:, :width], pre[:, width:]
    sigma = jax.nn.sigmoid(gate)
    first = per_device * model + j * width
    common = got_ref[here, first : first + width].astype(F32) * sigma
    gp_ref[here, at : at + width] = (common * upper * (1.0 + gate * (1.0 - sigma))).astype(BF16)
    gp_ref[here, at + width : at + hidden] = (common * gate).astype(BF16)


def grad_kernel(per_device, got_hbm, w_ref, gw_hbm, got_ref, gp_ref, gw_ref, sems):
    model, hidden = w_ref.shape[0], w_ref.shape[1] // per_device
    size, step, half = got_ref.shape[0], 256, 128
    start = starter(sems)
    got_in = iter(fetch_rows(start, got_hbm, got_ref, per_device, model, hidden // 2, step))
    outs = []
    for j in range(per_device):
        at = j * hidden
        for i in range(0, size, half):
            if i % step == 0:
                for copy in next(got_in):
                    copy.wait()
            swiglu_grads(got_ref, w_ref, gp_ref, per_device, j, i, half)
        for i in range(0, model, step):
            part = got_ref[:, j * model + i : j * model + i + step]
            gw_ref[i : i + step, at : at + hidden] = dot(part, gp_ref[:, at : at + hidden], ((0,), (0,))).astype(BF16)
            here = (pl.ds(i, step), pl.ds(at, hidden))
            outs.append(start(gw_ref.at[here], gw_hbm.at[here]))
    for copy in outs:
        copy.wait()


def route_kernel(per_device, got_hbm, w_ref, back_hbm, got_ref, gp_ref, back_ref, sems):
    model, hidden = w_ref.shape[0], w_ref.shape[1] // per_device
    size, step = got_ref.shape[0], 256
    start = starter(sems)
    got_in = iter(fetch_rows(start, got_hbm, got_ref, per_device, model, hidden // 2, step))
    outs = []
    for j in range(per_device):
        at = j * hidden
        for i in range(0, size, step):
            for copy in next(got_in):
                copy.wait()
            for half in (0, step // 2):
                swiglu_grads(got_ref, w_ref, gp_ref, per_device, j, i + half, step // 2)
            here = (pl.ds(i, step), pl.ds(j * model, model))
            rows = dot(gp_ref[i : i + step, at : at + hidden], w_ref[:, at : at + hidden], ((1,), (1,)))
            back_ref[i : i + step, j * model : (j + 1) * model] = rows.astype(BF16)
            outs.append(start(back_ref.at[here], back_hbm.at[here]))
    for copy in outs:
        copy.wait()


def sum_kernel(per_device, picks_ref, back_ref, out_ref):
    tok_count, model = out_ref.shape
    size = back_ref.shape[0]
    total = jnp.zeros((tok_count, model), F32)
    for j in range(per_device):
        total += dot(picks_ref[j * size : (j + 1) * size, :], back_ref[:, j * model : (j + 1) * model], ((0,), (0,)))
    out_ref[...] = total.astype(BF16)


STEPS = 10
NOTE_LANES = 128


def to_half(weights):
    wide = weights.astype(F32)
    top = jnp.max(jnp.abs(wide))
    bounds = jnp.array([2.0 ** (-10 * k) for k in range(1, STEPS + 1)], F32)
    lifts = jnp.array([2.0 ** (15 + 10 * k) for k in range(1, STEPS + 1)], F32)
    lift = jnp.max(jnp.where(top < bounds, lifts, 2.0**15))
    level = jnp.sum(jnp.where(top < bounds, 1.0, 0.0))
    note = jnp.broadcast_to(level, (weights.shape[0], NOTE_LANES))
    return jnp.concatenate([wide * lift, note], axis=1).astype(jnp.float16)


def from_half(gathered, shards):
    rows, lanes = gathered.shape[0], gathered.shape[1] - NOTE_LANES
    parts = gathered.reshape(shards, rows // shards, lanes + NOTE_LANES)
    level = parts[:, 0, lanes].astype(F32)[:, None]
    steps = jnp.arange(STEPS + 1, dtype=F32)[None, :]
    drops = jnp.array([2.0 ** (-15 - 10 * k) for k in range(STEPS + 1)], F32)[None, :]
    drop = jnp.sum(jnp.where(level == steps, drops, 0.0), axis=1)
    return (parts[:, :, :lanes].astype(F32) * drop[:, None, None]).astype(BF16).reshape(rows, lanes)


def call(kernel, outs, args, in_specs=None, out_specs=None, grid=(), scratch=(), flops=0, moved=0, room=VMEM_LIMIT):
    whole = pl.BlockSpec(memory_space=pltpu.VMEM)
    return pl.pallas_call(
        kernel,
        grid=grid,
        out_shape=[jax.ShapeDtypeStruct(s, t) for s, t in outs],
        in_specs=in_specs or [whole] * len(args),
        out_specs=out_specs or [whole] * len(outs),
        scratch_shapes=scratch,
        compiler_params=pltpu.CompilerParams(vmem_limit_bytes=room),
        cost_estimate=pl.CostEstimate(flops=flops, bytes_accessed=moved, transcendentals=0),
    )(*args)


def body(tokens, routes, route_gates, route_cotangent, gate_up):
    tok_count, topk = routes.shape
    width = route_cotangent.shape[2]
    model = tokens.shape[1]
    channels, per_device, hidden = gate_up.shape
    devices = lax.axis_size("expert")
    data_ways = lax.axis_size("dp")
    experts = per_device * devices
    cap = 3 * tok_count * topk // (2 * experts)
    size, count = devices * cap, tok_count * topk
    lanes = per_device * (model + width)
    vmem, hbm = pl.BlockSpec(memory_space=pltpu.VMEM), pl.BlockSpec(memory_space=pltpu.HBM)

    (packed,) = call(
        functools.partial(pack_kernel, per_device, devices, cap),
        [((size, lanes), BF16)],
        [routes.T, route_gates.T, tokens, route_cotangent.reshape(count, width)],
        in_specs=[hbm] * 4,
        out_specs=[hbm],
        scratch=[
            pltpu.VMEM((topk, tok_count), jnp.int32),
            pltpu.VMEM((topk, tok_count), F32),
            pltpu.VMEM((tok_count, model), BF16),
            pltpu.VMEM((count, width), BF16),
            pltpu.VMEM((count, width), BF16),
            pltpu.VMEM((size, lanes), BF16),
            pltpu.SemaphoreType.DMA((4 + 2 * (size // 256),)),
        ],
        flops=2 * per_device * size * (tok_count * model + count * width),
        moved=2 * size * lanes,
    )
    got = lax.all_to_all(packed, "expert", split_axis=0, concat_axis=0, tiled=True)
    later, _ = lax.optimization_barrier((gate_up, packed))
    sent = to_half(later.reshape(channels, per_device * hidden))
    full = from_half(lax.all_gather(sent, "dp", axis=0, tiled=True), data_ways)

    work = 2 * per_device * size * model * hidden
    tiles = size // 256
    held = [pltpu.VMEM((size, lanes), BF16), pltpu.VMEM((size, per_device * hidden), BF16)]
    (part,) = call(
        functools.partial(grad_kernel, per_device),
        [((model, per_device * hidden), BF16)],
        [got, full],
        in_specs=[hbm, vmem],
        out_specs=[hbm],
        scratch=[
            *held,
            pltpu.VMEM((model, per_device * hidden), BF16),
            pltpu.SemaphoreType.DMA((per_device * (2 * tiles + model // 256),)),
        ],
        flops=2 * work,
        moved=12 * size * model,
        room=ROOM,
    )
    mine = lax.psum_scatter(part, "dp", scatter_dimension=0, tiled=True)
    (back,) = call(
        functools.partial(route_kernel, per_device),
        [((size, per_device * model), BF16)],
        [got, full],
        in_specs=[hbm, vmem],
        out_specs=[hbm],
        scratch=[*held, pltpu.VMEM((size, per_device * model), BF16), pltpu.SemaphoreType.DMA((3 * per_device * tiles,))],
        flops=2 * work,
        moved=12 * size * model,
        room=ROOM,
    )
    later, _ = lax.optimization_barrier(((routes.T, route_gates.T), back))
    picks, sums = call(
        functools.partial(tally_kernel, per_device, devices, cap),
        [((per_device * size, tok_count), BF16), ((1, 128), F32)],
        later,
        moved=2 * per_device * size * tok_count,
    )
    returned = lax.all_to_all(back, "expert", split_axis=0, concat_axis=0, tiled=True)
    (grad_tokens,) = call(
        functools.partial(sum_kernel, per_device),
        [((tok_count, model), BF16)],
        [picks, returned],
        flops=2 * per_device * size * tok_count * model,
        moved=4 * size * model,
    )

    column = lax.psum(sums, "dp")[0, :experts].reshape(per_device, devices).T
    column = jnp.broadcast_to(column[:, :, None], (devices, per_device, 128)).reshape(devices, per_device * 128)
    column, _ = lax.optimization_barrier((column, returned))
    heard = lax.all_to_all(column, "expert", split_axis=0, concat_axis=0, tiled=True)
    totals = jnp.sum(heard, axis=0).reshape(per_device, 128)[:, 0]
    load = totals * (per_device / (tok_count * topk * data_ways))
    return (grad_tokens, mine.reshape(channels, per_device, hidden), load)


def solution(mesh):
    in_specs = (
        P(("dp", "expert"), None),
        P(("dp", "expert"), None),
        P(("dp", "expert"), None),
        P(("dp", "expert"), None, None),
        P("dp", "expert", None),
    )
    out_specs = (P(("dp", "expert"), None), P("dp", "expert", None), P("expert"))
    return jax.shard_map(body, mesh=mesh, in_specs=in_specs, out_specs=out_specs, check_vma=False)
```

```python
import functools

import jax
import jax.numpy as jnp
from jax import lax
from jax.experimental import pallas as pl
from jax.experimental.pallas import tpu as pltpu
from jax.sharding import PartitionSpec as P

F32 = jnp.float32
BF16 = jnp.bfloat16
VMEM_LIMIT = 60 * 1024 * 1024
ROOM = 32 * 1024 * 1024


def iota(shape, dim):
    return lax.broadcasted_iota(jnp.int32, shape, dim)


def dot(a, b, contract=((1,), (0,))):
    return lax.dot_general(a, b, (contract, ((), ())), preferred_element_type=F32)


def split3(x):
    high = x.astype(BF16)
    rest = x - high.astype(F32)
    middle = rest.astype(BF16)
    return high, middle, (rest - middle.astype(F32)).astype(BF16)


def slots_of(routes, per_device, devices):
    topk, tok_count = routes.shape
    row = iota((per_device * devices, 1), 0)
    expert = (row % devices) * per_device + row // devices
    hit = jnp.zeros((per_device * devices, tok_count), F32)
    for k in range(topk):
        hit = jnp.where(routes[k : k + 1, :] == expert, 1.0, hit)
    before = (iota((tok_count, tok_count), 0) < iota((tok_count, tok_count), 1)).astype(F32).astype(BF16)
    return expert, dot(hit.astype(BF16), before), hit > 0.5


def picks_of(tok_slot, cap):
    experts, tok_count = tok_slot.shape
    hits = tok_slot[:, None, :] == iota((experts, cap, tok_count), 1)
    return hits.astype(F32).reshape(experts * cap, tok_count).astype(BF16)


def pack_kernel(
    per_device, devices, cap, routes_hbm, gates_hbm, tokens_hbm, cot_hbm, out_hbm, routes_ref, gates_ref, tokens_ref, cot_ref, scaled_ref, out_ref, sems
):
    topk, tok_count = routes_ref.shape
    model, width = tokens_ref.shape[1], cot_ref.shape[1]
    count, size = tok_count * topk, devices * cap
    pairs = [(routes_hbm, routes_ref), (gates_hbm, gates_ref), (tokens_hbm, tokens_ref), (cot_hbm, cot_ref)]
    copies = [pltpu.make_async_copy(source, target, sems.at[i]) for i, (source, target) in enumerate(pairs)]
    for copy in copies:
        copy.start()

    spread = (iota((tok_count, count), 1) // topk == iota((tok_count, count), 0)).astype(F32).astype(BF16)
    copies[0].wait()
    copies[1].wait()
    wide = dot(routes_ref[...].astype(F32).astype(BF16), spread)
    own = iota((topk, count), 1) % topk == iota((topk, count), 0)
    routes = jnp.sum(jnp.where(own, wide, 0.0), axis=0, keepdims=True).astype(jnp.int32)
    own = iota((count, topk), 0) % topk == iota((count, topk), 1)
    tall = sum(dot(spread, part, ((0,), (1,))) for part in split3(gates_ref[...]))
    gates = jnp.sum(jnp.where(own, tall, 0.0), axis=1, keepdims=True)

    expert, earlier, named = slots_of(routes_ref[...], per_device, devices)
    tok_slot = jnp.where(named, earlier, -1.0).astype(jnp.int32)
    row = iota((per_device * devices, 1), 0)
    slots = jnp.where(routes == expert, (row * cap).astype(F32) + dot(earlier.astype(BF16), spread), 0.0)
    slot = jnp.sum(slots, axis=0, keepdims=True).astype(jnp.int32)
    picks = picks_of(tok_slot, cap)

    step = 256
    copies[2].wait()
    copies[3].wait()
    scaled_ref[...] = (cot_ref[...].astype(F32) * gates).astype(BF16)
    first = per_device * model
    outs = []

    def send(i, at, lanes):
        here = (pl.ds(i, step), pl.ds(at, lanes))
        outs.append(pltpu.make_async_copy(out_ref.at[here], out_hbm.at[here], sems.at[len(pairs) + len(outs)]))
        outs[-1].start()

    for i in range(0, size, step):
        for j in range(per_device):
            rows = dot(picks[j * size + i : j * size + i + step], tokens_ref[...])
            out_ref[i : i + step, j * model : (j + 1) * model] = rows.astype(BF16)
        send(i, 0, first)
        for j in range(per_device):
            hit = slot == iota((step, 1), 0) + (j * size + i)
            rows = dot(hit.astype(F32).astype(BF16), scaled_ref[...])
            out_ref[i : i + step, first + j * width : first + (j + 1) * width] = rows.astype(BF16)
        send(i, first, per_device * width)
    for copy in outs:
        copy.wait()


def tally_kernel(per_device, devices, cap, routes_ref, gates_ref, picks_ref, sums_ref):
    topk, tok_count = routes_ref.shape
    expert, earlier, named = slots_of(routes_ref[...], per_device, devices)
    picks_ref[...] = picks_of(jnp.where(named, earlier, -1.0).astype(jnp.int32), cap)
    mark = gates_ref[...].astype(BF16).astype(F32)
    sums = jnp.zeros((per_device * devices, 1), F32)
    for k in range(topk):
        chosen = jnp.where(routes_ref[k : k + 1, :] == expert, mark[k : k + 1, :], 0.0)
        sums += jnp.sum(chosen, axis=1, keepdims=True)
    row, lane = iota((per_device * devices, 128), 0), iota((per_device * devices, 128), 1)
    sums_ref[...] = jnp.sum(jnp.where(row == lane, sums, 0.0), axis=0, keepdims=True)


def starter(sems):
    copies = []

    def start(source, target):
        copies.append(pltpu.make_async_copy(source, target, sems.at[len(copies)]))
        copies[-1].start()
        return copies[-1]

    return start


def fetch_rows(start, got_hbm, got_ref, per_device, model, width, step):
    return [
        [
            start(got_hbm.at[pl.ds(i, step), pl.ds(at, count)], got_ref.at[pl.ds(i, step), pl.ds(at, count)])
            for at, count in ((j * model, model), (per_device * model + j * width, width))
        ]
        for j in range(per_device)
        for i in range(0, got_ref.shape[0], step)
    ]


def swiglu_grads(got_ref, w_ref, gp_ref, per_device, j, start, rows):
    model, hidden = w_ref.shape[0], w_ref.shape[1] // per_device
    width, here, at = hidden // 2, pl.ds(start, rows), j * hidden
    pre = dot(got_ref[here, j * model : (j + 1) * model], w_ref[:, at : at + hidden])
    gate, upper = pre[:, :width], pre[:, width:]
    sigma = jax.nn.sigmoid(gate)
    first = per_device * model + j * width
    common = got_ref[here, first : first + width].astype(F32) * sigma
    gp_ref[here, at : at + width] = (common * upper * (1.0 + gate * (1.0 - sigma))).astype(BF16)
    gp_ref[here, at + width : at + hidden] = (common * gate).astype(BF16)


def grad_kernel(per_device, got_hbm, w_ref, gw_hbm, got_ref, gp_ref, gw_ref, sems):
    model, hidden = w_ref.shape[0], w_ref.shape[1] // per_device
    size, step, half = got_ref.shape[0], 256, 128
    start = starter(sems)
    got_in = iter(fetch_rows(start, got_hbm, got_ref, per_device, model, hidden // 2, step))
    outs = []
    for j in range(per_device):
        at = j * hidden
        for i in range(0, size, half):
            if i % step == 0:
                for copy in next(got_in):
                    copy.wait()
            swiglu_grads(got_ref, w_ref, gp_ref, per_device, j, i, half)
        for i in range(0, model, step):
            part = got_ref[:, j * model + i : j * model + i + step]
            gw_ref[i : i + step, at : at + hidden] = dot(part, gp_ref[:, at : at + hidden], ((0,), (0,))).astype(BF16)
            here = (pl.ds(i, step), pl.ds(at, hidden))
            outs.append(start(gw_ref.at[here], gw_hbm.at[here]))
    for copy in outs:
        copy.wait()


def route_kernel(per_device, got_hbm, w_ref, back_hbm, got_ref, gp_ref, back_ref, sems):
    model, hidden = w_ref.shape[0], w_ref.shape[1] // per_device
    size, step = got_ref.shape[0], 256
    start = starter(sems)
    got_in = iter(fetch_rows(start, got_hbm, got_ref, per_device, model, hidden // 2, step))
    outs = []
    for j in range(per_device):
        at = j * hidden
        for i in range(0, size, step):
            for copy in next(got_in):
                copy.wait()
            for half in (0, step // 2):
                swiglu_grads(got_ref, w_ref, gp_ref, per_device, j, i + half, step // 2)
            here = (pl.ds(i, step), pl.ds(j * model, model))
            rows = dot(gp_ref[i : i + step, at : at + hidden], w_ref[:, at : at + hidden], ((1,), (1,)))
            back_ref[i : i + step, j * model : (j + 1) * model] = rows.astype(BF16)
            outs.append(start(back_ref.at[here], back_hbm.at[here]))
    for copy in outs:
        copy.wait()


def sum_kernel(per_device, picks_ref, back_ref, out_ref):
    tok_count, model = out_ref.shape
    size = back_ref.shape[0]
    total = jnp.zeros((tok_count, model), F32)
    for j in range(per_device):
        total += dot(picks_ref[j * size : (j + 1) * size, :], back_ref[:, j * model : (j + 1) * model], ((0,), (0,)))
    out_ref[...] = total.astype(BF16)


STEPS = 10
NOTE_LANES = 128


def lift_kernel(w_ref, out_ref):
    lanes = w_ref.shape[1]
    wide = w_ref[...].astype(F32)
    top = jnp.max(jnp.max(jnp.abs(wide), axis=0, keepdims=True), axis=1, keepdims=True)
    level, lift = jnp.zeros((1, 1), F32), jnp.full((1, 1), 2.0**15, F32)
    for k in range(1, STEPS + 1):
        level = jnp.where(top < 2.0 ** (-10 * k), float(k), level)
        lift = jnp.where(top < 2.0 ** (-10 * k), 2.0 ** (15 + 10 * k), lift)
    out_ref[:, :lanes] = (wide * lift).astype(BF16)
    out_ref[:, lanes:] = jnp.broadcast_to(level, (w_ref.shape[0], NOTE_LANES)).astype(BF16)


def from_half(gathered, shards):
    rows, lanes = gathered.shape[0], gathered.shape[1] - NOTE_LANES
    parts = gathered.reshape(shards, rows // shards, lanes + NOTE_LANES)
    level = jnp.max(parts[:, :8, lanes:].astype(F32), axis=(1, 2))[:, None]
    steps = jnp.arange(STEPS + 1, dtype=F32)[None, :]
    drops = jnp.array([2.0 ** (-15 - 10 * k) for k in range(STEPS + 1)], F32)[None, :]
    drop = jnp.sum(jnp.where(level == steps, drops, 0.0), axis=1)
    return (parts[:, :, :lanes].astype(F32) * drop[:, None, None]).astype(BF16).reshape(rows, lanes)


def call(kernel, outs, args, in_specs=None, out_specs=None, grid=(), scratch=(), flops=0, moved=0, room=VMEM_LIMIT):
    whole = pl.BlockSpec(memory_space=pltpu.VMEM)
    return pl.pallas_call(
        kernel,
        grid=grid,
        out_shape=[jax.ShapeDtypeStruct(s, t) for s, t in outs],
        in_specs=in_specs or [whole] * len(args),
        out_specs=out_specs or [whole] * len(outs),
        scratch_shapes=scratch,
        compiler_params=pltpu.CompilerParams(vmem_limit_bytes=room),
        cost_estimate=pl.CostEstimate(flops=flops, bytes_accessed=moved, transcendentals=0),
    )(*args)


def body(tokens, routes, route_gates, route_cotangent, gate_up):
    tok_count, topk = routes.shape
    width = route_cotangent.shape[2]
    model = tokens.shape[1]
    channels, per_device, hidden = gate_up.shape
    devices = lax.axis_size("expert")
    data_ways = lax.axis_size("dp")
    experts = per_device * devices
    cap = 3 * tok_count * topk // (2 * experts)
    size, count = devices * cap, tok_count * topk
    lanes = per_device * (model + width)
    vmem, hbm = pl.BlockSpec(memory_space=pltpu.VMEM), pl.BlockSpec(memory_space=pltpu.HBM)

    (packed,) = call(
        functools.partial(pack_kernel, per_device, devices, cap),
        [((size, lanes), BF16)],
        [routes.T, route_gates.T, tokens, route_cotangent.reshape(count, width)],
        in_specs=[hbm] * 4,
        out_specs=[hbm],
        scratch=[
            pltpu.VMEM((topk, tok_count), jnp.int32),
            pltpu.VMEM((topk, tok_count), F32),
            pltpu.VMEM((tok_count, model), BF16),
            pltpu.VMEM((count, width), BF16),
            pltpu.VMEM((count, width), BF16),
            pltpu.VMEM((size, lanes), BF16),
            pltpu.SemaphoreType.DMA((4 + 2 * (size // 256),)),
        ],
        flops=2 * per_device * size * (tok_count * model + count * width),
        moved=2 * size * lanes,
    )
    got = lax.all_to_all(packed, "expert", split_axis=0, concat_axis=0, tiled=True)
    later, _ = lax.optimization_barrier((gate_up, packed))
    (lifted,) = call(
        lift_kernel,
        [((channels, per_device * hidden + NOTE_LANES), BF16)],
        [later.reshape(channels, per_device * hidden)],
        moved=4 * channels * per_device * hidden,
        room=ROOM,
    )
    sent = lifted.astype(jnp.float16)
    full = from_half(lax.all_gather(sent, "dp", axis=0, tiled=True), data_ways)

    work = 2 * per_device * size * model * hidden
    tiles = size // 256
    held = [pltpu.VMEM((size, lanes), BF16), pltpu.VMEM((size, per_device * hidden), BF16)]
    (part,) = call(
        functools.partial(grad_kernel, per_device),
        [((model, per_device * hidden), BF16)],
        [got, full],
        in_specs=[hbm, vmem],
        out_specs=[hbm],
        scratch=[
            *held,
            pltpu.VMEM((model, per_device * hidden), BF16),
            pltpu.SemaphoreType.DMA((per_device * (2 * tiles + model // 256),)),
        ],
        flops=2 * work,
        moved=12 * size * model,
        room=ROOM,
    )
    mine = lax.psum_scatter(part, "dp", scatter_dimension=0, tiled=True)
    (back,) = call(
        functools.partial(route_kernel, per_device),
        [((size, per_device * model), BF16)],
        [got, full],
        in_specs=[hbm, vmem],
        out_specs=[hbm],
        scratch=[*held, pltpu.VMEM((size, per_device * model), BF16), pltpu.SemaphoreType.DMA((3 * per_device * tiles,))],
        flops=2 * work,
        moved=12 * size * model,
        room=ROOM,
    )
    later, _ = lax.optimization_barrier(((routes.T, route_gates.T), back))
    picks, sums = call(
        functools.partial(tally_kernel, per_device, devices, cap),
        [((per_device * size, tok_count), BF16), ((1, 128), F32)],
        later,
        moved=2 * per_device * size * tok_count,
    )
    returned = lax.all_to_all(back, "expert", split_axis=0, concat_axis=0, tiled=True)
    (grad_tokens,) = call(
        functools.partial(sum_kernel, per_device),
        [((tok_count, model), BF16)],
        [picks, returned],
        flops=2 * per_device * size * tok_count * model,
        moved=4 * size * model,
    )

    column = lax.psum(sums, "dp")[0, :experts].reshape(per_device, devices).T
    column = jnp.broadcast_to(column[:, :, None], (devices, per_device, 128)).reshape(devices, per_device * 128)
    column, _ = lax.optimization_barrier((column, returned))
    heard = lax.all_to_all(column, "expert", split_axis=0, concat_axis=0, tiled=True)
    totals = jnp.sum(heard, axis=0).reshape(per_device, 128)[:, 0]
    load = totals * (per_device / (tok_count * topk * data_ways))
    return (grad_tokens, mine.reshape(channels, per_device, hidden), load)


def solution(mesh):
    in_specs = (
        P(("dp", "expert"), None),
        P(("dp", "expert"), None),
        P(("dp", "expert"), None),
        P(("dp", "expert"), None, None),
        P("dp", "expert", None),
    )
    out_specs = (P(("dp", "expert"), None), P("dp", "expert", None), P("expert"))
    return jax.shard_map(body, mesh=mesh, in_specs=in_specs, out_specs=out_specs, check_vma=False)
```

```python
import functools

import jax
import jax.numpy as jnp
from jax import lax
from jax.experimental import pallas as pl
from jax.experimental.pallas import tpu as pltpu
from jax.sharding import PartitionSpec as P

F32 = jnp.float32
BF16 = jnp.bfloat16
VMEM_LIMIT = 60 * 1024 * 1024
ROOM = 32 * 1024 * 1024


def iota(shape, dim):
    return lax.broadcasted_iota(jnp.int32, shape, dim)


def dot(a, b, contract=((1,), (0,))):
    return lax.dot_general(a, b, (contract, ((), ())), preferred_element_type=F32)


def split3(x):
    high = x.astype(BF16)
    rest = x - high.astype(F32)
    middle = rest.astype(BF16)
    return high, middle, (rest - middle.astype(F32)).astype(BF16)


def slots_of(routes, per_device, devices):
    topk, tok_count = routes.shape
    row = iota((per_device * devices, 1), 0)
    expert = (row % devices) * per_device + row // devices
    hit = jnp.zeros((per_device * devices, tok_count), F32)
    for k in range(topk):
        hit = jnp.where(routes[k : k + 1, :] == expert, 1.0, hit)
    before = (iota((tok_count, tok_count), 0) < iota((tok_count, tok_count), 1)).astype(F32).astype(BF16)
    return expert, dot(hit.astype(BF16), before), hit > 0.5


def picks_of(tok_slot, cap):
    experts, tok_count = tok_slot.shape
    hits = tok_slot[:, None, :] == iota((experts, cap, tok_count), 1)
    return hits.astype(F32).reshape(experts * cap, tok_count).astype(BF16)


def pack_kernel(
    per_device, devices, cap, routes_hbm, gates_hbm, tokens_hbm, cot_hbm, out_hbm, routes_ref, gates_ref, tokens_ref, cot_ref, scaled_ref, out_ref, sems
):
    topk, tok_count = routes_ref.shape
    model, width = tokens_ref.shape[1], cot_ref.shape[1]
    count, size = tok_count * topk, devices * cap
    pairs = [(routes_hbm, routes_ref), (gates_hbm, gates_ref), (tokens_hbm, tokens_ref), (cot_hbm, cot_ref)]
    copies = [pltpu.make_async_copy(source, target, sems.at[i]) for i, (source, target) in enumerate(pairs)]
    for copy in copies:
        copy.start()

    spread = (iota((tok_count, count), 1) // topk == iota((tok_count, count), 0)).astype(F32).astype(BF16)
    copies[0].wait()
    copies[1].wait()
    wide = dot(routes_ref[...].astype(F32).astype(BF16), spread)
    own = iota((topk, count), 1) % topk == iota((topk, count), 0)
    routes = jnp.sum(jnp.where(own, wide, 0.0), axis=0, keepdims=True).astype(jnp.int32)
    own = iota((count, topk), 0) % topk == iota((count, topk), 1)
    tall = sum(dot(spread, part, ((0,), (1,))) for part in split3(gates_ref[...]))
    gates = jnp.sum(jnp.where(own, tall, 0.0), axis=1, keepdims=True)

    expert, earlier, named = slots_of(routes_ref[...], per_device, devices)
    tok_slot = jnp.where(named, earlier, -1.0).astype(jnp.int32)
    row = iota((per_device * devices, 1), 0)
    slots = jnp.where(routes == expert, (row * cap).astype(F32) + dot(earlier.astype(BF16), spread), 0.0)
    slot = jnp.sum(slots, axis=0, keepdims=True).astype(jnp.int32)
    picks = picks_of(tok_slot, cap)

    step = 256
    first = per_device * model
    outs = []

    def send(i, at, lanes):
        here = (pl.ds(i, step), pl.ds(at, lanes))
        outs.append(pltpu.make_async_copy(out_ref.at[here], out_hbm.at[here], sems.at[len(pairs) + len(outs)]))
        outs[-1].start()

    copies[2].wait()
    for i in range(0, size, step):
        for j in range(per_device):
            rows = dot(picks[j * size + i : j * size + i + step], tokens_ref[...])
            out_ref[i : i + step, j * model : (j + 1) * model] = rows.astype(BF16)
        send(i, 0, first)
    copies[3].wait()
    scaled_ref[...] = (cot_ref[...].astype(F32) * gates).astype(BF16)
    for i in range(0, size, step):
        for j in range(per_device):
            hit = slot == iota((step, 1), 0) + (j * size + i)
            rows = dot(hit.astype(F32).astype(BF16), scaled_ref[...])
            out_ref[i : i + step, first + j * width : first + (j + 1) * width] = rows.astype(BF16)
        send(i, first, per_device * width)
    for copy in outs:
        copy.wait()


def tally_kernel(per_device, devices, cap, routes_ref, gates_ref, picks_ref, sums_ref):
    topk, tok_count = routes_ref.shape
    expert, earlier, named = slots_of(routes_ref[...], per_device, devices)
    picks_ref[...] = picks_of(jnp.where(named, earlier, -1.0).astype(jnp.int32), cap)
    mark = gates_ref[...].astype(BF16).astype(F32)
    sums = jnp.zeros((per_device * devices, 1), F32)
    for k in range(topk):
        chosen = jnp.where(routes_ref[k : k + 1, :] == expert, mark[k : k + 1, :], 0.0)
        sums += jnp.sum(chosen, axis=1, keepdims=True)
    row, lane = iota((per_device * devices, 128), 0), iota((per_device * devices, 128), 1)
    sums_ref[...] = jnp.sum(jnp.where(row == lane, sums, 0.0), axis=0, keepdims=True)


def starter(sems):
    copies = []

    def start(source, target):
        copies.append(pltpu.make_async_copy(source, target, sems.at[len(copies)]))
        copies[-1].start()
        return copies[-1]

    return start


def fetch_rows(start, got_hbm, got_ref, per_device, model, width, step):
    return [
        [
            start(got_hbm.at[pl.ds(i, step), pl.ds(at, count)], got_ref.at[pl.ds(i, step), pl.ds(at, count)])
            for at, count in ((j * model, model), (per_device * model + j * width, width))
        ]
        for j in range(per_device)
        for i in range(0, got_ref.shape[0], step)
    ]


def swiglu_grads(got_ref, w_ref, gp_ref, per_device, j, start, rows):
    model, hidden = w_ref.shape[0], w_ref.shape[1] // per_device
    width, here, at = hidden // 2, pl.ds(start, rows), j * hidden
    pre = dot(got_ref[here, j * model : (j + 1) * model], w_ref[:, at : at + hidden])
    gate, upper = pre[:, :width], pre[:, width:]
    sigma = jax.nn.sigmoid(gate)
    first = per_device * model + j * width
    common = got_ref[here, first : first + width].astype(F32) * sigma
    gp_ref[here, at : at + width] = (common * upper * (1.0 + gate * (1.0 - sigma))).astype(BF16)
    gp_ref[here, at + width : at + hidden] = (common * gate).astype(BF16)


def grad_kernel(per_device, got_hbm, w_ref, gw_hbm, got_ref, gp_ref, gw_ref, sems):
    model, hidden = w_ref.shape[0], w_ref.shape[1] // per_device
    size, step, half = got_ref.shape[0], 256, 128
    start = starter(sems)
    got_in = iter(fetch_rows(start, got_hbm, got_ref, per_device, model, hidden // 2, step))
    outs = []
    for j in range(per_device):
        for i in range(0, size, half):
            if i % step == 0:
                for copy in next(got_in):
                    copy.wait()
            swiglu_grads(got_ref, w_ref, gp_ref, per_device, j, i, half)
    for j in range(per_device):
        at = j * hidden
        for i in range(0, model, step):
            part = got_ref[:, j * model + i : j * model + i + step]
            gw_ref[i : i + step, at : at + hidden] = dot(part, gp_ref[:, at : at + hidden], ((0,), (0,))).astype(BF16)
            here = (pl.ds(i, step), pl.ds(at, hidden))
            outs.append(start(gw_ref.at[here], gw_hbm.at[here]))
    for copy in outs:
        copy.wait()


def route_kernel(per_device, got_hbm, w_ref, back_hbm, got_ref, gp_ref, back_ref, sems):
    model, hidden = w_ref.shape[0], w_ref.shape[1] // per_device
    size, step = got_ref.shape[0], 256
    start = starter(sems)
    got_in = iter(fetch_rows(start, got_hbm, got_ref, per_device, model, hidden // 2, step))
    outs = []
    for j in range(per_device):
        at = j * hidden
        for i in range(0, size, step):
            for copy in next(got_in):
                copy.wait()
            for half in (0, step // 2):
                swiglu_grads(got_ref, w_ref, gp_ref, per_device, j, i + half, step // 2)
            here = (pl.ds(i, step), pl.ds(j * model, model))
            rows = dot(gp_ref[i : i + step, at : at + hidden], w_ref[:, at : at + hidden], ((1,), (1,)))
            back_ref[i : i + step, j * model : (j + 1) * model] = rows.astype(BF16)
            outs.append(start(back_ref.at[here], back_hbm.at[here]))
    for copy in outs:
        copy.wait()


def sum_kernel(per_device, picks_ref, back_ref, out_ref):
    tok_count, model = out_ref.shape
    size = back_ref.shape[0]
    total = jnp.zeros((tok_count, model), F32)
    for j in range(per_device):
        total += dot(picks_ref[j * size : (j + 1) * size, :], back_ref[:, j * model : (j + 1) * model], ((0,), (0,)))
    out_ref[...] = total.astype(BF16)


STEPS = 10
NOTE_LANES = 128


def lift_kernel(w_ref, out_ref):
    lanes = w_ref.shape[1]
    wide = w_ref[...].astype(F32)
    top = jnp.max(jnp.max(jnp.abs(wide), axis=0, keepdims=True), axis=1, keepdims=True)
    level, lift = jnp.zeros((1, 1), F32), jnp.full((1, 1), 2.0**15, F32)
    for k in range(1, STEPS + 1):
        level = jnp.where(top < 2.0 ** (-10 * k), float(k), level)
        lift = jnp.where(top < 2.0 ** (-10 * k), 2.0 ** (15 + 10 * k), lift)
    out_ref[:, :lanes] = (wide * lift).astype(BF16)
    out_ref[:, lanes:] = jnp.broadcast_to(level, (w_ref.shape[0], NOTE_LANES)).astype(BF16)


def from_half(gathered, shards):
    rows, lanes = gathered.shape[0], gathered.shape[1] - NOTE_LANES
    parts = gathered.reshape(shards, rows // shards, lanes + NOTE_LANES)
    level = jnp.max(parts[:, :8, lanes:].astype(F32), axis=(1, 2))[:, None]
    steps = jnp.arange(STEPS + 1, dtype=F32)[None, :]
    drops = jnp.array([2.0 ** (-15 - 10 * k) for k in range(STEPS + 1)], F32)[None, :]
    drop = jnp.sum(jnp.where(level == steps, drops, 0.0), axis=1)
    return (parts[:, :, :lanes].astype(F32) * drop[:, None, None]).astype(BF16).reshape(rows, lanes)


def call(kernel, outs, args, in_specs=None, out_specs=None, grid=(), scratch=(), flops=0, moved=0, room=VMEM_LIMIT):
    whole = pl.BlockSpec(memory_space=pltpu.VMEM)
    return pl.pallas_call(
        kernel,
        grid=grid,
        out_shape=[jax.ShapeDtypeStruct(s, t) for s, t in outs],
        in_specs=in_specs or [whole] * len(args),
        out_specs=out_specs or [whole] * len(outs),
        scratch_shapes=scratch,
        compiler_params=pltpu.CompilerParams(vmem_limit_bytes=room),
        cost_estimate=pl.CostEstimate(flops=flops, bytes_accessed=moved, transcendentals=0),
    )(*args)


def body(tokens, routes, route_gates, route_cotangent, gate_up):
    tok_count, topk = routes.shape
    width = route_cotangent.shape[2]
    model = tokens.shape[1]
    channels, per_device, hidden = gate_up.shape
    devices = lax.axis_size("expert")
    data_ways = lax.axis_size("dp")
    experts = per_device * devices
    cap = 3 * tok_count * topk // (2 * experts)
    size, count = devices * cap, tok_count * topk
    lanes = per_device * (model + width)
    vmem, hbm = pl.BlockSpec(memory_space=pltpu.VMEM), pl.BlockSpec(memory_space=pltpu.HBM)

    (packed,) = call(
        functools.partial(pack_kernel, per_device, devices, cap),
        [((size, lanes), BF16)],
        [routes.T, route_gates.T, tokens, route_cotangent.reshape(count, width)],
        in_specs=[hbm] * 4,
        out_specs=[hbm],
        scratch=[
            pltpu.VMEM((topk, tok_count), jnp.int32),
            pltpu.VMEM((topk, tok_count), F32),
            pltpu.VMEM((tok_count, model), BF16),
            pltpu.VMEM((count, width), BF16),
            pltpu.VMEM((count, width), BF16),
            pltpu.VMEM((size, lanes), BF16),
            pltpu.SemaphoreType.DMA((4 + 2 * (size // 256),)),
        ],
        flops=2 * per_device * size * (tok_count * model + count * width),
        moved=2 * size * lanes,
    )
    got = lax.all_to_all(packed, "expert", split_axis=0, concat_axis=0, tiled=True)
    later, _ = lax.optimization_barrier((gate_up, packed))
    (lifted,) = call(
        lift_kernel,
        [((channels, per_device * hidden + NOTE_LANES), BF16)],
        [later.reshape(channels, per_device * hidden)],
        moved=4 * channels * per_device * hidden,
        room=ROOM,
    )
    sent = lifted.astype(jnp.float16)
    full = from_half(lax.all_gather(sent, "dp", axis=0, tiled=True), data_ways)

    work = 2 * per_device * size * model * hidden
    tiles = size // 256
    held = [pltpu.VMEM((size, lanes), BF16), pltpu.VMEM((size, per_device * hidden), BF16)]
    (part,) = call(
        functools.partial(grad_kernel, per_device),
        [((model, per_device * hidden), BF16)],
        [got, full],
        in_specs=[hbm, vmem],
        out_specs=[hbm],
        scratch=[
            *held,
            pltpu.VMEM((model, per_device * hidden), BF16),
            pltpu.SemaphoreType.DMA((per_device * (2 * tiles + model // 256),)),
        ],
        flops=2 * work,
        moved=12 * size * model,
        room=ROOM,
    )
    mine = lax.psum_scatter(part, "dp", scatter_dimension=0, tiled=True)
    (back,) = call(
        functools.partial(route_kernel, per_device),
        [((size, per_device * model), BF16)],
        [got, full],
        in_specs=[hbm, vmem],
        out_specs=[hbm],
        scratch=[*held, pltpu.VMEM((size, per_device * model), BF16), pltpu.SemaphoreType.DMA((3 * per_device * tiles,))],
        flops=2 * work,
        moved=12 * size * model,
        room=ROOM,
    )
    later, _ = lax.optimization_barrier(((routes.T, route_gates.T), back))
    picks, sums = call(
        functools.partial(tally_kernel, per_device, devices, cap),
        [((per_device * size, tok_count), BF16), ((1, 128), F32)],
        later,
        moved=2 * per_device * size * tok_count,
    )
    returned = lax.all_to_all(back, "expert", split_axis=0, concat_axis=0, tiled=True)
    (grad_tokens,) = call(
        functools.partial(sum_kernel, per_device),
        [((tok_count, model), BF16)],
        [picks, returned],
        flops=2 * per_device * size * tok_count * model,
        moved=4 * size * model,
    )

    column = lax.psum(sums, "dp")[0, :experts].reshape(per_device, devices).T
    column = jnp.broadcast_to(column[:, :, None], (devices, per_device, 128)).reshape(devices, per_device * 128)
    column, _ = lax.optimization_barrier((column, returned))
    heard = lax.all_to_all(column, "expert", split_axis=0, concat_axis=0, tiled=True)
    totals = jnp.sum(heard, axis=0).reshape(per_device, 128)[:, 0]
    load = totals * (per_device / (tok_count * topk * data_ways))
    return (grad_tokens, mine.reshape(channels, per_device, hidden), load)


def solution(mesh):
    in_specs = (
        P(("dp", "expert"), None),
        P(("dp", "expert"), None),
        P(("dp", "expert"), None),
        P(("dp", "expert"), None, None),
        P("dp", "expert", None),
    )
    out_specs = (P(("dp", "expert"), None), P("dp", "expert", None), P("expert"))
    return jax.shard_map(body, mesh=mesh, in_specs=in_specs, out_specs=out_specs, check_vma=False)
```

```python
import functools

import jax
import jax.numpy as jnp
from jax import lax
from jax.experimental import pallas as pl
from jax.experimental.pallas import tpu as pltpu
from jax.sharding import PartitionSpec as P

F32 = jnp.float32
BF16 = jnp.bfloat16
VMEM_LIMIT = 60 * 1024 * 1024
ROOM = 32 * 1024 * 1024


def iota(shape, dim):
    return lax.broadcasted_iota(jnp.int32, shape, dim)


def dot(a, b, contract=((1,), (0,))):
    return lax.dot_general(a, b, (contract, ((), ())), preferred_element_type=F32)


def split3(x):
    high = x.astype(BF16)
    rest = x - high.astype(F32)
    middle = rest.astype(BF16)
    return high, middle, (rest - middle.astype(F32)).astype(BF16)


def slots_of(routes, per_device, devices):
    topk, tok_count = routes.shape
    row = iota((per_device * devices, 1), 0)
    expert = (row % devices) * per_device + row // devices
    hit = jnp.zeros((per_device * devices, tok_count), F32)
    for k in range(topk):
        hit = jnp.where(routes[k : k + 1, :] == expert, 1.0, hit)
    before = (iota((tok_count, tok_count), 0) < iota((tok_count, tok_count), 1)).astype(F32).astype(BF16)
    return expert, dot(hit.astype(BF16), before), hit > 0.5


def picks_of(tok_slot, cap):
    experts, tok_count = tok_slot.shape
    hits = tok_slot[:, None, :] == iota((experts, cap, tok_count), 1)
    return hits.astype(F32).reshape(experts * cap, tok_count).astype(BF16)


def pack_kernel(
    per_device, devices, cap, routes_hbm, gates_hbm, tokens_hbm, cot_hbm, out_hbm, routes_ref, gates_ref, tokens_ref, cot_ref, scaled_ref, out_ref, sems
):
    topk, tok_count = routes_ref.shape
    model, width = tokens_ref.shape[1], cot_ref.shape[1]
    count, size = tok_count * topk, devices * cap
    pairs = [(routes_hbm, routes_ref), (gates_hbm, gates_ref), (tokens_hbm, tokens_ref), (cot_hbm, cot_ref)]
    copies = [pltpu.make_async_copy(source, target, sems.at[i]) for i, (source, target) in enumerate(pairs)]
    for copy in copies:
        copy.start()

    spread = (iota((tok_count, count), 1) // topk == iota((tok_count, count), 0)).astype(F32).astype(BF16)
    copies[0].wait()
    copies[1].wait()
    wide = dot(routes_ref[...].astype(F32).astype(BF16), spread)
    own = iota((topk, count), 1) % topk == iota((topk, count), 0)
    routes = jnp.sum(jnp.where(own, wide, 0.0), axis=0, keepdims=True).astype(jnp.int32)
    own = iota((count, topk), 0) % topk == iota((count, topk), 1)
    tall = sum(dot(spread, part, ((0,), (1,))) for part in split3(gates_ref[...]))
    gates = jnp.sum(jnp.where(own, tall, 0.0), axis=1, keepdims=True)

    expert, earlier, named = slots_of(routes_ref[...], per_device, devices)
    tok_slot = jnp.where(named, earlier, -1.0).astype(jnp.int32)
    row = iota((per_device * devices, 1), 0)
    slots = jnp.where(routes == expert, (row * cap).astype(F32) + dot(earlier.astype(BF16), spread), 0.0)
    slot = jnp.sum(slots, axis=0, keepdims=True).astype(jnp.int32)
    picks = picks_of(tok_slot, cap)

    step = 256
    copies[2].wait()
    copies[3].wait()
    scaled_ref[...] = (cot_ref[...].astype(F32) * gates).astype(BF16)
    first = per_device * model
    outs = []

    def send(i, at, lanes):
        here = (pl.ds(i, step), pl.ds(at, lanes))
        outs.append(pltpu.make_async_copy(out_ref.at[here], out_hbm.at[here], sems.at[len(pairs) + len(outs)]))
        outs[-1].start()

    for i in range(0, size, step):
        for j in range(per_device):
            rows = dot(picks[j * size + i : j * size + i + step], tokens_ref[...])
            out_ref[i : i + step, j * model : (j + 1) * model] = rows.astype(BF16)
        send(i, 0, first)
        for j in range(per_device):
            near = jnp.clip(slot - (j * size + i), -1, step).astype(F32).astype(BF16)
            hit = jnp.where(near == iota((step, 1), 0).astype(F32).astype(BF16), jnp.bfloat16(1), jnp.bfloat16(0))
            rows = dot(hit, scaled_ref[...])
            out_ref[i : i + step, first + j * width : first + (j + 1) * width] = rows.astype(BF16)
        send(i, first, per_device * width)
    for copy in outs:
        copy.wait()


def tally_kernel(per_device, devices, cap, routes_ref, gates_ref, picks_ref, sums_ref):
    topk, tok_count = routes_ref.shape
    expert, earlier, named = slots_of(routes_ref[...], per_device, devices)
    picks_ref[...] = picks_of(jnp.where(named, earlier, -1.0).astype(jnp.int32), cap)
    mark = gates_ref[...].astype(BF16).astype(F32)
    sums = jnp.zeros((per_device * devices, 1), F32)
    for k in range(topk):
        chosen = jnp.where(routes_ref[k : k + 1, :] == expert, mark[k : k + 1, :], 0.0)
        sums += jnp.sum(chosen, axis=1, keepdims=True)
    row, lane = iota((per_device * devices, 128), 0), iota((per_device * devices, 128), 1)
    sums_ref[...] = jnp.sum(jnp.where(row == lane, sums, 0.0), axis=0, keepdims=True)


def starter(sems):
    copies = []

    def start(source, target):
        copies.append(pltpu.make_async_copy(source, target, sems.at[len(copies)]))
        copies[-1].start()
        return copies[-1]

    return start


def fetch_rows(start, got_hbm, got_ref, per_device, model, width, step):
    return [
        [
            start(got_hbm.at[pl.ds(i, step), pl.ds(at, count)], got_ref.at[pl.ds(i, step), pl.ds(at, count)])
            for at, count in ((j * model, model), (per_device * model + j * width, width))
        ]
        for j in range(per_device)
        for i in range(0, got_ref.shape[0], step)
    ]


def swiglu_grads(got_ref, w_ref, gp_ref, per_device, j, start, rows):
    model, hidden = w_ref.shape[0], w_ref.shape[1] // per_device
    width, here, at = hidden // 2, pl.ds(start, rows), j * hidden
    pre = dot(got_ref[here, j * model : (j + 1) * model], w_ref[:, at : at + hidden])
    gate, upper = pre[:, :width], pre[:, width:]
    sigma = jax.nn.sigmoid(gate)
    first = per_device * model + j * width
    common = got_ref[here, first : first + width].astype(F32) * sigma
    gp_ref[here, at : at + width] = (common * upper * (1.0 + gate * (1.0 - sigma))).astype(BF16)
    gp_ref[here, at + width : at + hidden] = (common * gate).astype(BF16)


def grad_kernel(per_device, got_hbm, w_ref, gw_hbm, got_ref, gp_ref, gw_ref, sems):
    model, hidden = w_ref.shape[0], w_ref.shape[1] // per_device
    size, step, half = got_ref.shape[0], 256, 128
    start = starter(sems)
    got_in = iter(fetch_rows(start, got_hbm, got_ref, per_device, model, hidden // 2, step))
    outs = []
    for j in range(per_device):
        at = j * hidden
        for i in range(0, size, half):
            if i % step == 0:
                for copy in next(got_in):
                    copy.wait()
            swiglu_grads(got_ref, w_ref, gp_ref, per_device, j, i, half)
        for i in range(0, model, step):
            part = got_ref[:, j * model + i : j * model + i + step]
            gw_ref[i : i + step, at : at + hidden] = dot(part, gp_ref[:, at : at + hidden], ((0,), (0,))).astype(BF16)
            here = (pl.ds(i, step), pl.ds(at, hidden))
            outs.append(start(gw_ref.at[here], gw_hbm.at[here]))
    for copy in outs:
        copy.wait()


def route_kernel(per_device, got_hbm, w_ref, back_hbm, got_ref, gp_ref, back_ref, sems):
    model, hidden = w_ref.shape[0], w_ref.shape[1] // per_device
    size, step = got_ref.shape[0], 256
    start = starter(sems)
    got_in = iter(fetch_rows(start, got_hbm, got_ref, per_device, model, hidden // 2, step))
    outs = []
    for j in range(per_device):
        at = j * hidden
        for i in range(0, size, step):
            for copy in next(got_in):
                copy.wait()
            for half in (0, step // 2):
                swiglu_grads(got_ref, w_ref, gp_ref, per_device, j, i + half, step // 2)
            here = (pl.ds(i, step), pl.ds(j * model, model))
            rows = dot(gp_ref[i : i + step, at : at + hidden], w_ref[:, at : at + hidden], ((1,), (1,)))
            back_ref[i : i + step, j * model : (j + 1) * model] = rows.astype(BF16)
            outs.append(start(back_ref.at[here], back_hbm.at[here]))
    for copy in outs:
        copy.wait()


def sum_kernel(per_device, picks_ref, back_ref, out_ref):
    tok_count, model = out_ref.shape
    size = back_ref.shape[0]
    total = jnp.zeros((tok_count, model), F32)
    for j in range(per_device):
        total += dot(picks_ref[j * size : (j + 1) * size, :], back_ref[:, j * model : (j + 1) * model], ((0,), (0,)))
    out_ref[...] = total.astype(BF16)


STEPS = 10
NOTE_LANES = 128


def lift_kernel(w_ref, out_ref):
    lanes = w_ref.shape[1]
    wide = w_ref[...].astype(F32)
    top = jnp.max(jnp.max(jnp.abs(wide), axis=0, keepdims=True), axis=1, keepdims=True)
    level, lift = jnp.zeros((1, 1), F32), jnp.full((1, 1), 2.0**15, F32)
    for k in range(1, STEPS + 1):
        level = jnp.where(top < 2.0 ** (-10 * k), float(k), level)
        lift = jnp.where(top < 2.0 ** (-10 * k), 2.0 ** (15 + 10 * k), lift)
    out_ref[:, :lanes] = (wide * lift).astype(BF16)
    out_ref[:, lanes:] = jnp.broadcast_to(level, (w_ref.shape[0], NOTE_LANES)).astype(BF16)


def from_half(gathered, shards):
    rows, lanes = gathered.shape[0], gathered.shape[1] - NOTE_LANES
    parts = gathered.reshape(shards, rows // shards, lanes + NOTE_LANES)
    level = jnp.max(parts[:, :8, lanes:].astype(F32), axis=(1, 2))[:, None]
    steps = jnp.arange(STEPS + 1, dtype=F32)[None, :]
    drops = jnp.array([2.0 ** (-15 - 10 * k) for k in range(STEPS + 1)], F32)[None, :]
    drop = jnp.sum(jnp.where(level == steps, drops, 0.0), axis=1)
    return (parts[:, :, :lanes].astype(F32) * drop[:, None, None]).astype(BF16).reshape(rows, lanes)


def call(kernel, outs, args, in_specs=None, out_specs=None, grid=(), scratch=(), flops=0, moved=0, room=VMEM_LIMIT):
    whole = pl.BlockSpec(memory_space=pltpu.VMEM)
    return pl.pallas_call(
        kernel,
        grid=grid,
        out_shape=[jax.ShapeDtypeStruct(s, t) for s, t in outs],
        in_specs=in_specs or [whole] * len(args),
        out_specs=out_specs or [whole] * len(outs),
        scratch_shapes=scratch,
        compiler_params=pltpu.CompilerParams(vmem_limit_bytes=room),
        cost_estimate=pl.CostEstimate(flops=flops, bytes_accessed=moved, transcendentals=0),
    )(*args)


def body(tokens, routes, route_gates, route_cotangent, gate_up):
    tok_count, topk = routes.shape
    width = route_cotangent.shape[2]
    model = tokens.shape[1]
    channels, per_device, hidden = gate_up.shape
    devices = lax.axis_size("expert")
    data_ways = lax.axis_size("dp")
    experts = per_device * devices
    cap = 3 * tok_count * topk // (2 * experts)
    size, count = devices * cap, tok_count * topk
    lanes = per_device * (model + width)
    vmem, hbm = pl.BlockSpec(memory_space=pltpu.VMEM), pl.BlockSpec(memory_space=pltpu.HBM)

    (packed,) = call(
        functools.partial(pack_kernel, per_device, devices, cap),
        [((size, lanes), BF16)],
        [routes.T, route_gates.T, tokens, route_cotangent.reshape(count, width)],
        in_specs=[hbm] * 4,
        out_specs=[hbm],
        scratch=[
            pltpu.VMEM((topk, tok_count), jnp.int32),
            pltpu.VMEM((topk, tok_count), F32),
            pltpu.VMEM((tok_count, model), BF16),
            pltpu.VMEM((count, width), BF16),
            pltpu.VMEM((count, width), BF16),
            pltpu.VMEM((size, lanes), BF16),
            pltpu.SemaphoreType.DMA((4 + 2 * (size // 256),)),
        ],
        flops=2 * per_device * size * (tok_count * model + count * width),
        moved=2 * size * lanes,
    )
    got = lax.all_to_all(packed, "expert", split_axis=0, concat_axis=0, tiled=True)
    later, _ = lax.optimization_barrier((gate_up, packed))
    (lifted,) = call(
        lift_kernel,
        [((channels, per_device * hidden + NOTE_LANES), BF16)],
        [later.reshape(channels, per_device * hidden)],
        moved=4 * channels * per_device * hidden,
        room=ROOM,
    )
    sent = lifted.astype(jnp.float16)
    full = from_half(lax.all_gather(sent, "dp", axis=0, tiled=True), data_ways)

    work = 2 * per_device * size * model * hidden
    tiles = size // 256
    held = [pltpu.VMEM((size, lanes), BF16), pltpu.VMEM((size, per_device * hidden), BF16)]
    (part,) = call(
        functools.partial(grad_kernel, per_device),
        [((model, per_device * hidden), BF16)],
        [got, full],
        in_specs=[hbm, vmem],
        out_specs=[hbm],
        scratch=[
            *held,
            pltpu.VMEM((model, per_device * hidden), BF16),
            pltpu.SemaphoreType.DMA((per_device * (2 * tiles + model // 256),)),
        ],
        flops=2 * work,
        moved=12 * size * model,
        room=ROOM,
    )
    mine = lax.psum_scatter(part, "dp", scatter_dimension=0, tiled=True)
    (back,) = call(
        functools.partial(route_kernel, per_device),
        [((size, per_device * model), BF16)],
        [got, full],
        in_specs=[hbm, vmem],
        out_specs=[hbm],
        scratch=[*held, pltpu.VMEM((size, per_device * model), BF16), pltpu.SemaphoreType.DMA((3 * per_device * tiles,))],
        flops=2 * work,
        moved=12 * size * model,
        room=ROOM,
    )
    later, _ = lax.optimization_barrier(((routes.T, route_gates.T), back))
    picks, sums = call(
        functools.partial(tally_kernel, per_device, devices, cap),
        [((per_device * size, tok_count), BF16), ((1, 128), F32)],
        later,
        moved=2 * per_device * size * tok_count,
    )
    returned = lax.all_to_all(back, "expert", split_axis=0, concat_axis=0, tiled=True)
    (grad_tokens,) = call(
        functools.partial(sum_kernel, per_device),
        [((tok_count, model), BF16)],
        [picks, returned],
        flops=2 * per_device * size * tok_count * model,
        moved=4 * size * model,
    )

    column = lax.psum(sums, "dp")[0, :experts].reshape(per_device, devices).T
    column = jnp.broadcast_to(column[:, :, None], (devices, per_device, 128)).reshape(devices, per_device * 128)
    column, _ = lax.optimization_barrier((column, returned))
    heard = lax.all_to_all(column, "expert", split_axis=0, concat_axis=0, tiled=True)
    totals = jnp.sum(heard, axis=0).reshape(per_device, 128)[:, 0]
    load = totals * (per_device / (tok_count * topk * data_ways))
    return (grad_tokens, mine.reshape(channels, per_device, hidden), load)


def solution(mesh):
    in_specs = (
        P(("dp", "expert"), None),
        P(("dp", "expert"), None),
        P(("dp", "expert"), None),
        P(("dp", "expert"), None, None),
        P("dp", "expert", None),
    )
    out_specs = (P(("dp", "expert"), None), P("dp", "expert", None), P("expert"))
    return jax.shard_map(body, mesh=mesh, in_specs=in_specs, out_specs=out_specs, check_vma=False)
```
